32 devices in a mesh: groups: 2 (over x), blk: 16 (over z, y, core).
Axes of the slice: x: 2, y: 2, z: 4, core: 2. Of those that a mesh axis runs over, the one named last changes fastest.
Arguments:
- query: bfloat16 [8192, 1024], P(('groups', 'blk')), parts along dimension 0, may hold values from -5 to 5
- key_in: bfloat16 [8192, 1024], P(('groups', 'blk')), parts along dimension 0, may hold values from -6 to 6
- value: bfloat16 [8192, 1024], P(('groups', 'blk')), parts along dimension 0, may hold values from -6 to 6
- grad_out: bfloat16 [8192, 1024], P(('groups', 'blk')), parts along dimension 0, may hold values from -6 to 6
- neighbors: int32 [64, 8], P(('groups', 'blk')), parts along dimension 0, may hold values from 0 to 31, as said below
- counts: int32 [64], P(('groups', 'blk')), parts along dimension 0, may hold values from 2 to 8, as said below
Outputs:
- attn_out: bfloat16 [8192, 1024], P(('groups', 'blk')), parts along dimension 0
- grad_query: bfloat16 [8192, 1024], P(('groups', 'blk')), parts along dimension 0
- grad_key: bfloat16 [8192, 1024], P(('groups', 'blk')), parts along dimension 0
- grad_value: bfloat16 [8192, 1024], P(('groups', 'blk')), parts along dimension 0
The draws below stay inside these ranges and needn't reach their ends.
There are 2 independent parts, one for each index of `groups`. The reference program is written for one: setup_inputs(seed, part) draws one part's arguments, and reference() takes and returns one part's arrays. A program takes and returns all parts, laid end to end along the dimension named above; each array names one. Nothing has to cross between parts.
Inputs may be any that keep to these rules, and one draw needn't show every extreme that they name: `neighbors`: row b holds 8 distinct block indices; its first entry is b itself; every entry is a block whose device (block // 2) is at most 2 steps from b's device along blk, counted cyclically; only the first counts[b] entries are used. `counts`: some block has exactly 8 and some exactly 2.
All inputs are finite; a program needn't handle non-finite values.
Results may differ from the reference program's by a relative error of at most 0.0086.
Values may be sent and summed in bfloat16 or wider, within the bound.
A program may use at most 128 MiB of HBM per device.

```python
import math
import jax
import jax.numpy as jnp
from jax import lax

HEADS = 16
HDIM = 64
D = 1024
BLOCK = 128
BLK_DEV = 2
NB = 8
REACH = 2
BLOCKS = 32
NODES = 4096


def draw_query(key, part):
    model_width = HEADS * HDIM
    entries = jnp.clip(jax.random.normal(jax.random.fold_in(key, 1), (NODES, model_width), jnp.float32), -5.0, 5.0)
    return entries.astype(jnp.bfloat16)


def draw_key_in(key, part):
    model_width = HEADS * HDIM
    entries = jnp.clip(jax.random.normal(jax.random.fold_in(key, 3), (NODES, model_width), jnp.float32), -6.0, 6.0)
    return entries.astype(jnp.bfloat16)


def draw_neighbors(key, part):
    shard_count = BLOCKS // BLK_DEV
    span_blocks = (2 * REACH + 1) * BLK_DEV
    block_ids = jnp.arange(BLOCKS)
    home = block_ids // BLK_DEV
    window_ids = jnp.arange(span_blocks)
    window_blocks = jnp.mod(home[:, None] - REACH + window_ids[None, :] // BLK_DEV, shard_count) * BLK_DEV + window_ids[None, :] % BLK_DEV
    own_slot = REACH * BLK_DEV + block_ids % BLK_DEV
    ranking = jax.random.randint(jax.random.fold_in(key, 11), (BLOCKS, span_blocks), 0, 1 << 20) * span_blocks + window_ids[None, :]
    ranking = jnp.where(window_ids[None, :] == own_slot[:, None], -1, ranking)
    picked = jnp.argsort(ranking, axis=1)[:, :NB]
    return jnp.take_along_axis(window_blocks, picked, axis=1).astype(jnp.int32)


def draw_counts(key, part):
    shard_count = BLOCKS // BLK_DEV
    block_ids = jnp.arange(BLOCKS)
    base = jax.random.randint(jax.random.fold_in(key, 21), (BLOCKS,), 2, NB + 1)
    heavy = jax.random.randint(jax.random.fold_in(key, 22), (shard_count,), 0, 8) == 0
    base = jnp.where(jnp.repeat(heavy, BLK_DEV), NB, base)
    fullest = jax.random.randint(jax.random.fold_in(key, 23), (), 0, BLOCKS)
    lowest = jnp.mod(fullest + 1 + jax.random.randint(jax.random.fold_in(key, 24), (), 0, BLOCKS - 1), BLOCKS)
    base = jnp.where(block_ids == fullest, NB, base)
    base = jnp.where(block_ids == lowest, 2, base)
    return base.astype(jnp.int32)


def steps_of(key, dims, pieces, least, high):
    gain = 1.0
    for axis_at, shards_of in pieces:
        draws = jax.random.uniform(jax.random.fold_in(jax.random.fold_in(key, 6), axis_at), (shards_of,), jnp.float32, least / len(pieces), high / len(pieces))
        gain = gain * jnp.repeat(jnp.exp(draws), dims[axis_at] // shards_of).reshape((-1,) + (1,) * (len(dims) - 1 - axis_at))
    return gain


def normal_values(stream_key, dims, width, bound, shards=(), held_as=jnp.bfloat16):
    factor_of = steps_of(stream_key, dims, shards, -0.22, 0.18) if shards else 1.0
    values = jax.random.normal(stream_key, dims, jnp.float32) * width * factor_of
    return jnp.minimum(jnp.maximum(values, -bound), bound).astype(held_as)


def setup_inputs(seed: int = 0, part: int = 0) -> dict:
    splits = jax.random.split(jax.random.key(seed), 7)
    part_splits = jax.random.split(jax.random.fold_in(splits[6], part), 7)
    query = draw_query(jax.random.fold_in(jax.random.fold_in(splits[6], part), 71), part)
    key_in = draw_key_in(jax.random.fold_in(jax.random.fold_in(splits[6], part), 71), part)
    value = normal_values(part_splits[2], (NODES, D), 1.0, 6.0, ((0, 16),))
    grad_out = normal_values(part_splits[3], (NODES, D), 1.0, 6.0, ((0, 16),))
    neighbors = draw_neighbors(jax.random.fold_in(jax.random.fold_in(splits[6], part), 71), part)
    counts = draw_counts(jax.random.fold_in(jax.random.fold_in(splits[6], part), 71), part)
    return dict(query=query, key_in=key_in, value=value, grad_out=grad_out, neighbors=neighbors, counts=counts)


def split_heads(matrix):
    return matrix.reshape(matrix.shape[0], HEADS, HDIM).astype(jnp.float32)

def merge_heads(matrix):
    return matrix.reshape(matrix.shape[0], HEADS * HDIM)

def reference(query, key_in, value, grad_out, neighbors, counts):
    factor = 1.0 / math.sqrt(HDIM)
    model_width = HEADS * HDIM
    q_blocks = query.reshape(BLOCKS, BLOCK, model_width)
    k_blocks = key_in.reshape(BLOCKS, BLOCK, model_width)
    v_blocks = value.reshape(BLOCKS, BLOCK, model_width)
    g_blocks = grad_out.reshape(BLOCKS, BLOCK, model_width)
    slot_ids = jnp.arange(NB, dtype=jnp.int32)

    def block_tiles(blk_id):
        chosen = neighbors[blk_id]
        k_all = split_heads(k_blocks[chosen].reshape(NB * BLOCK, model_width))
        v_all = split_heads(v_blocks[chosen].reshape(NB * BLOCK, model_width))
        live_keys = jnp.repeat(slot_ids < counts[blk_id], BLOCK)
        q_tile = split_heads(q_blocks[blk_id])
        scores = jnp.einsum('qhd,khd->hqk', q_tile, k_all) * factor
        scores = jnp.where(live_keys[None, None, :], scores, -jnp.inf)
        row_max = lax.optimization_barrier(jnp.max(scores, axis=2, keepdims=True))
        exponent = jnp.exp(scores - row_max)
        soft_probs = exponent / lax.optimization_barrier(jnp.sum(exponent, axis=2, keepdims=True))
        rounded = lax.optimization_barrier(soft_probs.astype(jnp.bfloat16)).astype(jnp.float32)
        return (chosen, q_tile, k_all, v_all, soft_probs, rounded)

    def forward(blk_id):
        chosen, q_tile, k_all, v_all, soft_probs, rounded = block_tiles(blk_id)
        mixed_out = jnp.einsum('hqk,khd->qhd', rounded, v_all)
        return merge_heads(mixed_out).astype(jnp.bfloat16)
    attn_out = lax.map(forward, jnp.arange(BLOCKS, dtype=jnp.int32)).reshape(NODES, model_width)
    row_delta = lax.optimization_barrier(jnp.sum(split_heads(grad_out) * split_heads(attn_out), axis=2))
    delta_blocks = row_delta.reshape(BLOCKS, BLOCK, HEADS)

    def backward(state_in, blk_id):
        grad_k, grad_v = state_in
        chosen, q_tile, k_all, v_all, soft_probs, rounded = block_tiles(blk_id)
        g_tile = split_heads(g_blocks[blk_id])
        dprobs = jnp.einsum('qhd,khd->hqk', g_tile, v_all)
        dscores = soft_probs * (dprobs - delta_blocks[blk_id].T[:, :, None])
        dscores = lax.optimization_barrier(dscores.astype(jnp.bfloat16)).astype(jnp.float32)
        grad_q = jnp.einsum('hqk,khd->qhd', dscores, k_all) * factor
        dv_part = jnp.einsum('hqk,qhd->khd', rounded, g_tile).reshape(NB, BLOCK, model_width)
        dk_part = (jnp.einsum('hqk,qhd->khd', dscores, q_tile) * factor).reshape(NB, BLOCK, model_width)
        grad_k = grad_k.at[chosen].add(dk_part)
        grad_v = grad_v.at[chosen].add(dv_part)
        return ((grad_k, grad_v), merge_heads(grad_q).astype(jnp.bfloat16))
    zeros_all = jnp.zeros((BLOCKS, BLOCK, model_width), jnp.float32)
    (grad_k, grad_v), grad_q = lax.scan(backward, (zeros_all, zeros_all), jnp.arange(BLOCKS, dtype=jnp.int32))
    grad_query = grad_q.reshape(NODES, model_width)
    grad_key = grad_k.reshape(NODES, model_width).astype(jnp.bfloat16)
    grad_value = grad_v.reshape(NODES, model_width).astype(jnp.bfloat16)
    return (attn_out, grad_query, grad_key, grad_value)
```

```python
import functools
import math

import jax
import jax.numpy as jnp
from jax import lax
from jax.experimental import pallas as pl
from jax.experimental.pallas import tpu as pltpu
from jax.sharding import PartitionSpec as P

HEADS = 16
LANES = 128
AHEAD = 4
SLOTS = 5
MASKED = -1e30
F32 = jnp.float32
BF16 = jnp.bfloat16


def matmul(a, b):
    return jnp.dot(a, b, preferred_element_type=F32)


def matmul_nt(a, b):
    return lax.dot_general(a, b, (((1,), (1,)), ((), ())), preferred_element_type=F32)


def kernel(
    shards, own_blocks, list_width, head_dim,
    nbr_ref, cnt_ref, q_ref, k_ref, v_ref, g_ref,
    out_ref, dq_ref, dk_ref, dv_ref,
    kv, acc, sib_s, sib_r, far_s, far_r, near_s, near_r,
    bias, s_scr, e_scr, d_scr, sends, recvs,
):
    rows, width = q_ref.shape
    chunks = width // LANES
    pack = LANES // head_dim
    blk_len = rows // own_blocks
    factor = 1.0 / math.sqrt(head_dim)
    chips = shards // 2

    me = lax.axis_index("blk")
    core = lax.rem(me, 2)
    chip = lax.div(me, 2)
    odd = lax.rem(chip, 2)
    step = 1 - 2 * odd
    near_chip = chip + step
    far_chip = lax.rem(chip - step + chips, chips)
    ahead_chip = lax.rem(chip + 2 * step + chips, chips)
    back_chip = lax.rem(chip - 2 * step + chips, chips)
    sibling = 2 * chip + 1 - core
    near = 2 * near_chip + core
    ahead = 2 * ahead_chip + core
    back = 2 * back_chip + core
    mix = lax.rem(core + chip, 2)
    lent = 2 + mix

    barrier = pltpu.get_barrier_semaphore()
    for other in (sibling, near, ahead, back):
        pl.semaphore_signal(
            barrier, inc=1, device_id={"blk": other}, device_id_type=pl.DeviceIdType.MESH
        )

    for c in range(chunks):
        kv[0, c, 0] = k_ref[:, c * LANES:(c + 1) * LANES]
        kv[0, c, 1] = v_ref[:, c * LANES:(c + 1) * LANES]

    row_id = lax.broadcasted_iota(jnp.int32, bias.shape, 0)
    lane_blk = lax.broadcasted_iota(jnp.int32, bias.shape, 1) // blk_len
    borrowed_chip = near_chip * mix + far_chip * (1 - mix)
    borrowed = 2 * borrowed_chip + 1 - core
    key_blk = jnp.full(bias.shape, -2, jnp.int32)
    for slot, dev in enumerate((me, sibling, near, 2 * far_chip + core, borrowed)):
        for b in range(own_blocks):
            key_blk = jnp.where(row_id == slot * own_blocks + b, dev * own_blocks + b, key_blk)
    allowed = jnp.zeros(bias.shape, jnp.int32)
    for s in range(list_width):
        entry = jnp.full(bias.shape, -1, jnp.int32)
        for b in range(own_blocks):
            live = jnp.where(s < cnt_ref[b], nbr_ref[b, s], -1)
            entry = jnp.where(lane_blk == b, live, entry)
        allowed = jnp.where(entry == key_blk, 1, allowed)
    bias[...] = jnp.where(allowed == 1, 0.0, MASKED).astype(F32)

    pl.semaphore_wait(barrier, 4)

    def remote(stream, src, dst, c, dev):
        return pltpu.make_async_remote_copy(
            src_ref=src,
            dst_ref=dst,
            send_sem=sends.at[stream, c],
            recv_sem=recvs.at[stream, c],
            device_id={"blk": dev},
            device_id_type=pl.DeviceIdType.MESH,
        )

    def to_near(c):
        return remote(0, kv.at[0, c], kv.at[2, c], c, near)

    def to_sibling(c):
        return remote(1, kv.at[0, c], kv.at[1, c], c, sibling)

    def relay(c):
        return remote(2, kv.at[2, c], kv.at[3, c], c, ahead)

    def lend(c):
        return remote(3, kv.at[lent, c], kv.at[4, c], c, sibling)

    def grad_sibling(c):
        return remote(4, sib_s.at[c], sib_r.at[c], c, sibling)

    def grad_far(c):
        return remote(5, far_s.at[c], far_r.at[c], c, back)

    def grad_near(c):
        return remote(6, near_s.at[c], near_r.at[c], c, near)

    def compute(c):
        cols = pl.ds(pl.multiple_of(c * LANES, LANES), LANES)
        q_t = q_ref[:, cols].T
        g_t = g_ref[:, cols].T
        out_parts, dq_parts, qs_parts, gs_parts = [], [], [], []
        for h in range(pack):
            lo, hi = h * head_dim, (h + 1) * head_dim

            def padded(x):
                pieces = []
                if lo:
                    pieces.append(jnp.zeros((lo, rows), x.dtype))
                pieces.append(x)
                if hi < LANES:
                    pieces.append(jnp.zeros((LANES - hi, rows), x.dtype))
                return jnp.concatenate(pieces, axis=0)

            q_h = q_t[lo:hi]
            g_h = g_t[lo:hi]
            q_pad = padded(q_h)
            g_pad = padded(g_h)
            here = slice(h * rows, (h + 1) * rows)
            top = None
            for slot in range(SLOTS):
                scores = matmul(kv[slot, c, 0], q_pad)
                for b in range(own_blocks):
                    r = slot * own_blocks + b
                    part = scores[b * blk_len:(b + 1) * blk_len] + bias[r:r + 1, :]
                    s_scr[r * blk_len:(r + 1) * blk_len, :] = part
                    part_top = jnp.max(part, axis=0, keepdims=True)
                    top = part_top if top is None else jnp.maximum(top, part_top)
            total = jnp.zeros((1, rows), F32)
            mixed = jnp.zeros((head_dim, rows), F32)
            for slot in range(SLOTS):
                at = slice(slot * rows, (slot + 1) * rows)
                e = jnp.exp2((s_scr[at, :] - top) * (factor * math.log2(math.e)))
                total = total + jnp.sum(e, axis=0, keepdims=True)
                e_b = e.astype(BF16)
                e_scr[at, here] = e_b
                mixed = mixed + matmul(kv[slot, c, 1].T[lo:hi], e_b)
            inv = 1.0 / total
            out_h = (mixed * inv).astype(BF16)
            g_f = g_h.astype(F32)
            delta = jnp.sum(g_f * out_h.astype(F32), axis=0, keepdims=True)
            dq = jnp.zeros((head_dim, rows), F32)
            for slot in range(SLOTS):
                at = slice(slot * rows, (slot + 1) * rows)
                dprobs = matmul(kv[slot, c, 1], g_pad)
                d_b = (e_scr[at, here].astype(F32) * (dprobs - delta)).astype(BF16)
                d_scr[at, here] = d_b
                dq = dq + matmul(kv[slot, c, 0].T[lo:hi], d_b)
            out_parts.append(out_h)
            dq_parts.append((dq * (inv * factor)).astype(BF16))
            gs_parts.append(padded((g_f * inv).astype(BF16)))
            qs_parts.append(padded((q_h.astype(F32) * (inv * factor)).astype(BF16)))
        out_ref[:, cols] = jnp.concatenate(out_parts, axis=0).T
        dq_ref[:, cols] = jnp.concatenate(dq_parts, axis=0).T
        q_all = jnp.concatenate(qs_parts, axis=1)
        g_all = jnp.concatenate(gs_parts, axis=1)
        for slot in range(SLOTS):
            at = slice(slot * rows, (slot + 1) * rows)
            dk = matmul_nt(d_scr[at, :], q_all)
            dv = matmul_nt(e_scr[at, :], g_all)
            if slot in (1, 4):
                sib_s[c, slot // 4, 0] = dk.astype(BF16)
                sib_s[c, slot // 4, 1] = dv.astype(BF16)
            else:
                acc[c, max(slot - 1, 0), 0] = dk
                acc[c, max(slot - 1, 0), 1] = dv

    for c in range(AHEAD):
        to_near(c).start()
        to_sibling(c).start()

    def body(t, carry):
        @pl.when(t + AHEAD < chunks)
        def _():
            to_near(t + AHEAD).start()
            to_sibling(t + AHEAD).start()

        @pl.when(t < chunks)
        def _():
            to_near(t).wait_recv()
            relay(t).start()

        @pl.when((t >= 1) & (t < chunks + 1))
        def _():
            relay(t - 1).wait_recv()
            lend(t - 1).start()

        @pl.when((t >= 3) & (t < chunks + 3))
        def _():
            c = t - 3
            grad_sibling(c).wait_recv()
            acc[c, lent - 1] += sib_r[c, 1].astype(F32)
            far_s[c] = acc[c, 2].astype(BF16)
            grad_far(c).start()

        @pl.when((t >= 4) & (t < chunks + 4))
        def _():
            c = t - 4
            grad_far(c).wait_recv()
            near_s[c] = (acc[c, 1] + far_r[c].astype(F32)).astype(BF16)
            grad_near(c).start()

        @pl.when(t >= 5)
        def _():
            c = t - 5
            cols = pl.ds(pl.multiple_of(c * LANES, LANES), LANES)
            grad_near(c).wait_recv()
            final = acc[c, 0] + sib_r[c, 0].astype(F32) + near_r[c].astype(F32)
            dk_ref[:, cols] = final[0].astype(BF16)
            dv_ref[:, cols] = final[1].astype(BF16)

        @pl.when((t >= 2) & (t < chunks + 2))
        def _():
            c = t - 2
            to_sibling(c).wait_recv()
            lend(c).wait_recv()
            compute(c)
            grad_sibling(c).start()

        return carry

    lax.fori_loop(0, chunks + 5, body, 0)

    def finish(c, carry):
        for copy in (to_near, to_sibling, relay, lend, grad_sibling, grad_far, grad_near):
            copy(c).wait_send()
        return carry

    lax.fori_loop(0, chunks, finish, 0)


def local(shards, query, key_in, value, grad_out, neighbors, counts):
    rows, width = query.shape
    own_blocks, list_width = neighbors.shape
    head_dim = width // HEADS
    chunks = width // LANES
    pack = LANES // head_dim
    tile = (2, rows, LANES)
    vmem = pl.BlockSpec(memory_space=pltpu.VMEM)
    smem = pl.BlockSpec(memory_space=pltpu.SMEM)
    shape = jax.ShapeDtypeStruct((rows, width), query.dtype)
    bias_rows = -(-SLOTS * own_blocks // 8) * 8
    return pl.pallas_call(
        functools.partial(kernel, shards, own_blocks, list_width, head_dim),
        out_shape=(shape,) * 4,
        in_specs=[smem, smem, vmem, vmem, vmem, vmem],
        out_specs=(vmem,) * 4,
        scratch_shapes=[
            pltpu.VMEM((SLOTS, chunks) + tile, BF16),
            pltpu.VMEM((chunks, 3) + tile, F32),
            pltpu.VMEM((chunks, 2) + tile, BF16),
            pltpu.VMEM((chunks, 2) + tile, BF16),
            pltpu.VMEM((chunks,) + tile, BF16),
            pltpu.VMEM((chunks,) + tile, BF16),
            pltpu.VMEM((chunks,) + tile, BF16),
            pltpu.VMEM((chunks,) + tile, BF16),
            pltpu.VMEM((bias_rows, rows), F32),
            pltpu.VMEM((SLOTS * rows, rows), F32),
            pltpu.VMEM((SLOTS * rows, pack * rows), BF16),
            pltpu.VMEM((SLOTS * rows, pack * rows), BF16),
            pltpu.SemaphoreType.DMA((7, chunks)),
            pltpu.SemaphoreType.DMA((7, chunks)),
        ],
        compiler_params=pltpu.CompilerParams(
            collective_id=0, has_side_effects=True, vmem_limit_bytes=52 * 1024 * 1024
        ),
        name="graph_attention",
    )(neighbors, counts, query, key_in, value, grad_out)


def solution(mesh):
    rows = P(("groups", "blk"), None)
    return jax.shard_map(
        functools.partial(local, mesh.shape["blk"]),
        mesh=mesh,
        in_specs=(rows, rows, rows, rows, rows, P(("groups", "blk"))),
        out_specs=(rows,) * 4,
        check_vma=False,
    )
```

```python
import functools
import math

import jax
import jax.numpy as jnp
from jax import lax
from jax.experimental import pallas as pl
from jax.experimental.pallas import tpu as pltpu
from jax.sharding import PartitionSpec as P

HEADS = 16
LANES = 128
AHEAD = 4
SLOTS = 5
MASKED = -1e30
F32 = jnp.float32
BF16 = jnp.bfloat16


def matmul(a, b):
    return jnp.dot(a, b, preferred_element_type=F32)


def matmul_nt(a, b):
    return lax.dot_general(a, b, (((1,), (1,)), ((), ())), preferred_element_type=F32)


def kernel(
    shards, own_blocks, list_width, head_dim,
    nbr_ref, cnt_ref, q_ref, k_ref, v_ref, g_ref,
    out_ref, dq_ref, dk_ref, dv_ref,
    kv, acc, sib_s, sib_r, far_s, far_r, near_s, near_r,
    bias, s_scr, e_scr, d_scr, kt_scr, vt_scr, q_scr, g_scr, sends, recvs, loads,
):
    rows, width = q_ref.shape
    chunks = width // LANES
    pack = LANES // head_dim
    blk_len = rows // own_blocks
    factor = 1.0 / math.sqrt(head_dim)
    chips = shards // 2

    me = lax.axis_index("blk")
    core = lax.rem(me, 2)
    chip = lax.div(me, 2)
    odd = lax.rem(chip, 2)
    step = 1 - 2 * odd
    near_chip = chip + step
    far_chip = lax.rem(chip - step + chips, chips)
    ahead_chip = lax.rem(chip + 2 * step + chips, chips)
    back_chip = lax.rem(chip - 2 * step + chips, chips)
    sibling = 2 * chip + 1 - core
    near = 2 * near_chip + core
    ahead = 2 * ahead_chip + core
    back = 2 * back_chip + core
    mix = lax.rem(core + chip, 2)
    lent = 2 + mix

    barrier = pltpu.get_barrier_semaphore()
    for other in (sibling, near, ahead, back):
        pl.semaphore_signal(
            barrier, inc=1, device_id={"blk": other}, device_id_type=pl.DeviceIdType.MESH
        )

    def load(which, c):
        cols = pl.ds(pl.multiple_of(c * LANES, LANES), LANES)
        source = (k_ref, v_ref)[which]
        return pltpu.make_async_copy(
            source.at[:, cols], kv.at[0, c, which], loads.at[which, c]
        )

    load_q = pltpu.make_async_copy(q_ref, q_scr, loads.at[2, 0])
    load_g = pltpu.make_async_copy(g_ref, g_scr, loads.at[2, 1])
    for c in range(chunks):
        load(0, c).start()
        load(1, c).start()
    load_q.start()
    load_g.start()

    row_id = lax.broadcasted_iota(jnp.int32, bias.shape, 0)
    lane_blk = lax.broadcasted_iota(jnp.int32, bias.shape, 1) // blk_len
    borrowed_chip = near_chip * mix + far_chip * (1 - mix)
    borrowed = 2 * borrowed_chip + 1 - core
    key_blk = jnp.full(bias.shape, -2, jnp.int32)
    for slot, dev in enumerate((me, sibling, near, 2 * far_chip + core, borrowed)):
        for b in range(own_blocks):
            key_blk = jnp.where(row_id == slot * own_blocks + b, dev * own_blocks + b, key_blk)
    allowed = jnp.zeros(bias.shape, jnp.int32)
    for s in range(list_width):
        entry = jnp.full(bias.shape, -1, jnp.int32)
        for b in range(own_blocks):
            live = jnp.where(s < cnt_ref[b], nbr_ref[b, s], -1)
            entry = jnp.where(lane_blk == b, live, entry)
        allowed = jnp.where(entry == key_blk, 1, allowed)
    bias[...] = jnp.where(allowed == 1, 0.0, MASKED).astype(F32)

    pl.semaphore_wait(barrier, 4)

    def remote(stream, src, dst, c, dev):
        return pltpu.make_async_remote_copy(
            src_ref=src,
            dst_ref=dst,
            send_sem=sends.at[stream, c],
            recv_sem=recvs.at[stream, c],
            device_id={"blk": dev},
            device_id_type=pl.DeviceIdType.MESH,
        )

    def to_near(c):
        return remote(0, kv.at[0, c], kv.at[2, c], c, near)

    def to_sibling(c):
        return remote(1, kv.at[0, c], kv.at[1, c], c, sibling)

    def relay(c):
        return remote(2, kv.at[2, c], kv.at[3, c], c, ahead)

    def lend(c):
        return remote(3, kv.at[lent, c], kv.at[4, c], c, sibling)

    def grad_sibling(c):
        return remote(4, sib_s.at[c], sib_r.at[c], c, sibling)

    def grad_far(c):
        return remote(5, far_s.at[c], far_r.at[c], c, back)

    def grad_near(c):
        return remote(6, near_s.at[c], near_r.at[c], c, near)

    def compute(c):
        cols = pl.ds(pl.multiple_of(c * LANES, LANES), LANES)
        q_t = q_scr[:, cols].T
        g_t = g_scr[:, cols].T
        keys = kv[:, c, 0].reshape(SLOTS * rows, LANES)
        vals = kv[:, c, 1].reshape(SLOTS * rows, LANES)
        for slot in range(SLOTS):
            at = slice(slot * rows, (slot + 1) * rows)
            kt_scr[:, at] = kv[slot, c, 0].T
            vt_scr[:, at] = kv[slot, c, 1].T

        def padded(x, h):
            pieces = []
            if h:
                pieces.append(jnp.zeros((h * head_dim, rows), x.dtype))
            pieces.append(x)
            if h < pack - 1:
                pieces.append(jnp.zeros(((pack - 1 - h) * head_dim, rows), x.dtype))
            return jnp.concatenate(pieces, axis=0)

        heads = [slice(h * head_dim, (h + 1) * head_dim) for h in range(pack)]
        out_parts, dq_parts, qs_parts, gs_parts = [], [], [], []
        for h in range(pack):
            s_scr[h] = matmul(keys, padded(q_t[heads[h]], h))
        for h in range(pack):
            here = slice(h * rows, (h + 1) * rows)
            top = None
            for r in range(SLOTS * own_blocks):
                part = jnp.max(s_scr[h, r * blk_len:(r + 1) * blk_len, :], axis=0, keepdims=True)
                part = part + bias[r:r + 1, :]
                top = part if top is None else jnp.maximum(top, part)
            total = jnp.zeros((1, rows), F32)
            for r in range(SLOTS * own_blocks):
                at = slice(r * blk_len, (r + 1) * blk_len)
                shift = top - bias[r:r + 1, :]
                e = jnp.exp2((s_scr[h, at, :] - shift) * (factor * math.log2(math.e)))
                total = total + jnp.sum(e, axis=0, keepdims=True)
                e_scr[at, here] = e.astype(BF16)
            mixed = matmul(vt_scr[heads[h], :], e_scr[:, here])
            inv = 1.0 / total
            out_h = (mixed * inv).astype(BF16)
            g_f = g_t[heads[h]].astype(F32)
            delta = jnp.sum(g_f * out_h.astype(F32), axis=0, keepdims=True)
            dprobs = matmul(vals, padded(g_t[heads[h]], h))
            d_scr[:, here] = (e_scr[:, here].astype(F32) * (dprobs - delta)).astype(BF16)
            dq = matmul(kt_scr[heads[h], :], d_scr[:, here])
            out_parts.append(out_h)
            dq_parts.append((dq * (inv * factor)).astype(BF16))
            gs_parts.append(padded((g_f * inv).astype(BF16), h))
            qs_parts.append(padded((q_t[heads[h]].astype(F32) * (inv * factor)).astype(BF16), h))
        out_ref[:, cols] = jnp.concatenate(out_parts, axis=0).T
        dq_ref[:, cols] = jnp.concatenate(dq_parts, axis=0).T
        dk = matmul_nt(d_scr[...], jnp.concatenate(qs_parts, axis=1))
        dv = matmul_nt(e_scr[...], jnp.concatenate(gs_parts, axis=1))
        for slot in range(SLOTS):
            at = slice(slot * rows, (slot + 1) * rows)
            if slot in (1, 4):
                sib_s[c, slot // 4, 0] = dk[at].astype(BF16)
                sib_s[c, slot // 4, 1] = dv[at].astype(BF16)
            else:
                acc[c, max(slot - 1, 0), 0] = dk[at]
                acc[c, max(slot - 1, 0), 1] = dv[at]

    def publish(c):
        load(0, c).wait()
        load(1, c).wait()
        to_near(c).start()
        to_sibling(c).start()

    for c in range(AHEAD):
        publish(c)
    load_q.wait()
    load_g.wait()

    def body(t, carry):
        @pl.when(t + AHEAD < chunks)
        def _():
            publish(t + AHEAD)

        @pl.when(t < chunks)
        def _():
            to_near(t).wait_recv()
            relay(t).start()

        @pl.when((t >= 1) & (t < chunks + 1))
        def _():
            relay(t - 1).wait_recv()
            lend(t - 1).start()

        @pl.when((t >= 3) & (t < chunks + 3))
        def _():
            c = t - 3
            grad_sibling(c).wait_recv()
            acc[c, lent - 1] += sib_r[c, 1].astype(F32)
            far_s[c] = acc[c, 2].astype(BF16)
            grad_far(c).start()

        @pl.when((t >= 4) & (t < chunks + 4))
        def _():
            c = t - 4
            grad_far(c).wait_recv()
            near_s[c] = (acc[c, 1] + far_r[c].astype(F32)).astype(BF16)
            grad_near(c).start()

        @pl.when(t >= 5)
        def _():
            c = t - 5
            cols = pl.ds(pl.multiple_of(c * LANES, LANES), LANES)
            grad_near(c).wait_recv()
            final = acc[c, 0] + sib_r[c, 0].astype(F32) + near_r[c].astype(F32)
            dk_ref[:, cols] = final[0].astype(BF16)
            dv_ref[:, cols] = final[1].astype(BF16)

        @pl.when((t >= 2) & (t < chunks + 2))
        def _():
            c = t - 2
            to_sibling(c).wait_recv()
            lend(c).wait_recv()
            compute(c)
            grad_sibling(c).start()

        return carry

    lax.fori_loop(0, chunks + 5, body, 0)

    def finish(c, carry):
        for copy in (to_near, to_sibling, relay, lend, grad_sibling, grad_far, grad_near):
            copy(c).wait_send()
        return carry

    lax.fori_loop(0, chunks, finish, 0)


def hand_over(*refs):
    sems = refs[-1]
    copies = [pltpu.make_async_copy(refs[i], refs[4 + i], sems.at[i]) for i in range(4)]
    for copy in copies:
        copy.start()
    for copy in copies:
        copy.wait()


def local(shards, query, key_in, value, grad_out, neighbors, counts):
    rows, width = query.shape
    own_blocks, list_width = neighbors.shape
    head_dim = width // HEADS
    chunks = width // LANES
    pack = LANES // head_dim
    tile = (2, rows, LANES)
    vmem = pl.BlockSpec(memory_space=pltpu.VMEM)
    hbm = pl.BlockSpec(memory_space=pl.ANY)
    smem = pl.BlockSpec(memory_space=pltpu.SMEM)
    shape = jax.ShapeDtypeStruct((rows, width), query.dtype)
    bias_rows = -(-SLOTS * own_blocks // 8) * 8
    results = pl.pallas_call(
        functools.partial(kernel, shards, own_blocks, list_width, head_dim),
        out_shape=(shape,) * 4,
        in_specs=[smem, smem, hbm, hbm, hbm, hbm],
        out_specs=(vmem,) * 4,
        scratch_shapes=[
            pltpu.VMEM((SLOTS, chunks) + tile, BF16),
            pltpu.VMEM((chunks, 3) + tile, F32),
            pltpu.VMEM((chunks, 2) + tile, BF16),
            pltpu.VMEM((chunks, 2) + tile, BF16),
            pltpu.VMEM((chunks,) + tile, BF16),
            pltpu.VMEM((chunks,) + tile, BF16),
            pltpu.VMEM((chunks,) + tile, BF16),
            pltpu.VMEM((chunks,) + tile, BF16),
            pltpu.VMEM((bias_rows, rows), F32),
            pltpu.VMEM((pack, SLOTS * rows, rows), F32),
            pltpu.VMEM((SLOTS * rows, pack * rows), BF16),
            pltpu.VMEM((SLOTS * rows, pack * rows), BF16),
            pltpu.VMEM((LANES, SLOTS * rows), BF16),
            pltpu.VMEM((LANES, SLOTS * rows), BF16),
            pltpu.VMEM((rows, width), BF16),
            pltpu.VMEM((rows, width), BF16),
            pltpu.SemaphoreType.DMA((7, chunks)),
            pltpu.SemaphoreType.DMA((7, chunks)),
            pltpu.SemaphoreType.DMA((3, chunks)),
        ],
        compiler_params=pltpu.CompilerParams(
            collective_id=0, has_side_effects=True, vmem_limit_bytes=56 * 1024 * 1024
        ),
        name="graph_attention",
    )(neighbors, counts, query, key_in, value, grad_out)
    return pl.pallas_call(
        hand_over,
        out_shape=(shape,) * 4,
        in_specs=[hbm] * 4,
        out_specs=(hbm,) * 4,
        scratch_shapes=[pltpu.SemaphoreType.DMA((4,))],
        compiler_params=pltpu.CompilerParams(vmem_limit_bytes=60 * 1024 * 1024),
        name="hand_over",
    )(*results)


def solution(mesh):
    rows = P(("groups", "blk"), None)
    return jax.shard_map(
        functools.partial(local, mesh.shape["blk"]),
        mesh=mesh,
        in_specs=(rows, rows, rows, rows, rows, P(("groups", "blk"))),
        out_specs=(rows,) * 4,
        check_vma=False,
    )
```

```python
import functools
import math

import jax
import jax.numpy as jnp
from jax import lax
from jax.experimental import pallas as pl
from jax.experimental.pallas import tpu as pltpu
from jax.sharding import PartitionSpec as P

HEADS = 16
LANES = 128
AHEAD = 3
SLOTS = 5
MASKED = -1e30
F32 = jnp.float32
BF16 = jnp.bfloat16


def matmul(a, b):
    return jnp.dot(a, b, preferred_element_type=F32)


def matmul_nt(a, b):
    return lax.dot_general(a, b, (((1,), (1,)), ((), ())), preferred_element_type=F32)


def kernel(
    shards, own_blocks, list_width, head_dim,
    nbr_ref, cnt_ref, q_ref, k_ref, v_ref, g_ref,
    out_ref, dq_ref, dk_ref, dv_ref,
    kv, acc, sib_s, sib_r, far_s, far_r, near_s, near_r,
    bias, s_scr, e_scr, d_scr, kt_scr, vt_scr, q_scr, g_scr,
    q_t, g_t, out_t, dq_t, qs_scr, gs_scr, sends, recvs, loads,
):
    rows, width = q_ref.shape
    chunks = width // LANES
    pack = LANES // head_dim
    blk_len = rows // own_blocks
    factor = 1.0 / math.sqrt(head_dim)
    chips = shards // 2

    me = lax.axis_index("blk")
    core = lax.rem(me, 2)
    chip = lax.div(me, 2)
    odd = lax.rem(chip, 2)
    step = 1 - 2 * odd
    near_chip = chip + step
    far_chip = lax.rem(chip - step + chips, chips)
    ahead_chip = lax.rem(chip + 2 * step + chips, chips)
    back_chip = lax.rem(chip - 2 * step + chips, chips)
    sibling = 2 * chip + 1 - core
    near = 2 * near_chip + core
    ahead = 2 * ahead_chip + core
    back = 2 * back_chip + core
    mix = lax.rem(core + chip, 2)
    lent = 2 + mix

    barrier = pltpu.get_barrier_semaphore()
    for other in (sibling, near, ahead, back):
        pl.semaphore_signal(
            barrier, inc=1, device_id={"blk": other}, device_id_type=pl.DeviceIdType.MESH
        )

    def load(which, c):
        cols = pl.ds(pl.multiple_of(c * LANES, LANES), LANES)
        source = (k_ref, v_ref)[which]
        return pltpu.make_async_copy(
            source.at[:, cols], kv.at[0, c, which], loads.at[which, c]
        )

    load_q = pltpu.make_async_copy(q_ref, q_scr, loads.at[2, 0])
    load_g = pltpu.make_async_copy(g_ref, g_scr, loads.at[2, 1])
    for c in range(chunks):
        load(0, c).start()
        load(1, c).start()
    load_q.start()
    load_g.start()

    row_id = lax.broadcasted_iota(jnp.int32, bias.shape, 0)
    lane_blk = lax.broadcasted_iota(jnp.int32, bias.shape, 1) // blk_len
    borrowed_chip = near_chip * mix + far_chip * (1 - mix)
    borrowed = 2 * borrowed_chip + 1 - core
    key_blk = jnp.full(bias.shape, -2, jnp.int32)
    for slot, dev in enumerate((me, sibling, near, 2 * far_chip + core, borrowed)):
        for b in range(own_blocks):
            key_blk = jnp.where(row_id == slot * own_blocks + b, dev * own_blocks + b, key_blk)
    allowed = jnp.zeros(bias.shape, jnp.int32)
    for s in range(list_width):
        entry = jnp.full(bias.shape, -1, jnp.int32)
        for b in range(own_blocks):
            live = jnp.where(s < cnt_ref[b], nbr_ref[b, s], -1)
            entry = jnp.where(lane_blk == b, live, entry)
        allowed = jnp.where(entry == key_blk, 1, allowed)
    bias[...] = jnp.where(allowed == 1, 0.0, MASKED).astype(F32)

    pl.semaphore_wait(barrier, 4)

    def remote(stream, src, dst, c, part, dev):
        return pltpu.make_async_remote_copy(
            src_ref=src,
            dst_ref=dst,
            send_sem=sends.at[stream, part, c],
            recv_sem=recvs.at[stream, part, c],
            device_id={"blk": dev},
            device_id_type=pl.DeviceIdType.MESH,
        )

    def to_near(c, part):
        return remote(0, kv.at[0, c, part], kv.at[2, c, part], c, part, near)

    def to_sibling(c, part):
        return remote(1, kv.at[0, c, part], kv.at[1, c, part], c, part, sibling)

    def relay(c, part):
        return remote(2, kv.at[2, c, part], kv.at[3, c, part], c, part, ahead)

    def lend(c, part):
        return remote(3, kv.at[lent, c, part], kv.at[4, c, part], c, part, sibling)

    def grad_sibling(c, part):
        return remote(4, sib_s.at[c, part], sib_r.at[c, part], c, part, sibling)

    def grad_far(c, part):
        return remote(5, far_s.at[c, part], far_r.at[c, part], c, part, back)

    def grad_near(c, part):
        return remote(6, near_s.at[c, part], near_r.at[c, part], c, part, near)

    def columns(c):
        return pl.ds(pl.multiple_of(c * LANES, LANES), LANES)

    def publish(c):
        for part in range(2):
            load(part, c).wait()
            to_near(c, part).start()
            to_sibling(c, part).start()

    def pass_on(c):
        for part in range(2):
            to_near(c, part).wait_recv()
            relay(c, part).start()

    def lend_on(c):
        for part in range(2):
            relay(c, part).wait_recv()
            lend(c, part).start()

    def send_far(c):
        for part in range(2):
            grad_sibling(c, part).wait_recv()
            acc[c, lent - 1, part] += sib_r[c, part, 1].astype(F32)
            far_s[c, part] = acc[c, 2, part].astype(BF16)
            grad_far(c, part).start()

    def send_near(c):
        for part in range(2):
            grad_far(c, part).wait_recv()
            near_s[c, part] = (acc[c, 1, part] + far_r[c, part].astype(F32)).astype(BF16)
            grad_near(c, part).start()

    def close(c):
        for part, result in enumerate((dk_ref, dv_ref)):
            grad_near(c, part).wait_recv()
            final = acc[c, 0, part] + sib_r[c, part, 0].astype(F32)
            result[:, columns(c)] = (final + near_r[c, part].astype(F32)).astype(BF16)

    def exchange(c):
        @pl.when(c + AHEAD < chunks)
        def _():
            publish(c + AHEAD)

        @pl.when(c + 2 < chunks)
        def _():
            pass_on(c + 2)

        @pl.when(c + 1 < chunks)
        def _():
            lend_on(c + 1)

        @pl.when(c >= 1)
        def _():
            send_far(c - 1)

        @pl.when(c >= 2)
        def _():
            send_near(c - 2)

        @pl.when(c >= 3)
        def _():
            close(c - 3)

    def padded(x, h):
        pieces = []
        if h:
            pieces.append(jnp.zeros((h * head_dim, rows), x.dtype))
        pieces.append(x)
        if h < pack - 1:
            pieces.append(jnp.zeros(((pack - 1 - h) * head_dim, rows), x.dtype))
        return jnp.concatenate(pieces, axis=0)

    def one_head(c, h):
        head = slice(h * head_dim, (h + 1) * head_dim)
        here = slice(h * rows, (h + 1) * rows)
        keys = kv[:, c, 0].reshape(SLOTS * rows, LANES)
        vals = kv[:, c, 1].reshape(SLOTS * rows, LANES)
        q_h = q_t[head, :]
        g_h = g_t[head, :]
        s_scr[h] = matmul(keys, padded(q_h, h))
        top = None
        for r in range(SLOTS * own_blocks):
            part = jnp.max(s_scr[h, r * blk_len:(r + 1) * blk_len, :], axis=0, keepdims=True)
            part = part + bias[r:r + 1, :]
            top = part if top is None else jnp.maximum(top, part)
        total = jnp.zeros((1, rows), F32)
        for r in range(SLOTS * own_blocks):
            at = slice(r * blk_len, (r + 1) * blk_len)
            shift = top - bias[r:r + 1, :]
            e = jnp.exp2((s_scr[h, at, :] - shift) * (factor * math.log2(math.e)))
            total = total + jnp.sum(e, axis=0, keepdims=True)
            e_scr[at, here] = e.astype(BF16)
        mixed = matmul(vt_scr[head, :], e_scr[:, here])
        inv = 1.0 / total
        out_h = (mixed * inv).astype(BF16)
        g_f = g_h.astype(F32)
        delta = jnp.sum(g_f * out_h.astype(F32), axis=0, keepdims=True)
        dprobs = matmul(vals, padded(g_h, h))
        d_scr[:, here] = (e_scr[:, here].astype(F32) * (dprobs - delta)).astype(BF16)
        dq = matmul(kt_scr[head, :], d_scr[:, here])
        out_t[head, :] = out_h
        dq_t[head, :] = (dq * (inv * factor)).astype(BF16)
        gs_scr[:, here] = padded((g_f * inv).astype(BF16), h)
        qs_scr[:, here] = padded((q_h.astype(F32) * (inv * factor)).astype(BF16), h)

    for c in range(AHEAD):
        publish(c)
    load_q.wait()
    load_g.wait()
    pass_on(0)
    pass_on(1)
    lend_on(0)

    def body(c, carry):
        cols = columns(c)
        q_t[...] = q_scr[:, cols].T
        g_t[...] = g_scr[:, cols].T
        for part in range(2):
            to_sibling(c, part).wait_recv()
            lend(c, part).wait_recv()
        for slot in range(SLOTS):
            at = slice(slot * rows, (slot + 1) * rows)
            kt_scr[:, at] = kv[slot, c, 0].T
            vt_scr[:, at] = kv[slot, c, 1].T
        for h in range(pack):
            if h == pack // 2:
                exchange(c)
            one_head(c, h)
        for part, (left, right) in enumerate(((d_scr, qs_scr), (e_scr, gs_scr))):
            grad = matmul_nt(left[...], right[...])
            for slot in range(SLOTS):
                at = slice(slot * rows, (slot + 1) * rows)
                if slot in (1, 4):
                    sib_s[c, part, slot // 4] = grad[at].astype(BF16)
                else:
                    acc[c, max(slot - 1, 0), part] = grad[at]
            grad_sibling(c, part).start()
        out_ref[:, cols] = out_t[...].T
        dq_ref[:, cols] = dq_t[...].T
        return carry

    lax.fori_loop(0, chunks, body, 0)

    send_far(chunks - 1)
    send_near(chunks - 2)
    close(chunks - 3)
    send_near(chunks - 1)
    close(chunks - 2)
    close(chunks - 1)

    def finish(c, carry):
        for copy in (to_near, to_sibling, relay, lend, grad_sibling, grad_far, grad_near):
            for part in range(2):
                copy(c, part).wait_send()
        return carry

    lax.fori_loop(0, chunks, finish, 0)


def hand_over(*refs):
    sources, results, held, sems = refs[:4], refs[4:8], refs[8], refs[9]
    reads = [pltpu.make_async_copy(sources[i], held.at[i], sems.at[0, i]) for i in range(4)]
    writes = [pltpu.make_async_copy(held.at[i], results[i], sems.at[1, i]) for i in range(4)]
    for read in reads:
        read.start()
    for read, write in zip(reads, writes):
        read.wait()
        write.start()
    for write in writes:
        write.wait()


def local(shards, query, key_in, value, grad_out, neighbors, counts):
    rows, width = query.shape
    own_blocks, list_width = neighbors.shape
    head_dim = width // HEADS
    chunks = width // LANES
    pack = LANES // head_dim
    tile = (2, rows, LANES)
    vmem = pl.BlockSpec(memory_space=pltpu.VMEM)
    hbm = pl.BlockSpec(memory_space=pl.ANY)
    smem = pl.BlockSpec(memory_space=pltpu.SMEM)
    shape = jax.ShapeDtypeStruct((rows, width), query.dtype)
    bias_rows = -(-SLOTS * own_blocks // 8) * 8
    results = pl.pallas_call(
        functools.partial(kernel, shards, own_blocks, list_width, head_dim),
        out_shape=(shape,) * 4,
        in_specs=[smem, smem, hbm, hbm, hbm, hbm],
        out_specs=(vmem,) * 4,
        scratch_shapes=[
            pltpu.VMEM((SLOTS, chunks) + tile, BF16),
            pltpu.VMEM((chunks, 3) + tile, F32),
            pltpu.VMEM((chunks, 2) + tile, BF16),
            pltpu.VMEM((chunks, 2) + tile, BF16),
            pltpu.VMEM((chunks,) + tile, BF16),
            pltpu.VMEM((chunks,) + tile, BF16),
            pltpu.VMEM((chunks,) + tile, BF16),
            pltpu.VMEM((chunks,) + tile, BF16),
            pltpu.VMEM((bias_rows, rows), F32),
            pltpu.VMEM((pack, SLOTS * rows, rows), F32),
            pltpu.VMEM((SLOTS * rows, pack * rows), BF16),
            pltpu.VMEM((SLOTS * rows, pack * rows), BF16),
            pltpu.VMEM((LANES, SLOTS * rows), BF16),
            pltpu.VMEM((LANES, SLOTS * rows), BF16),
            pltpu.VMEM((rows, width), BF16),
            pltpu.VMEM((rows, width), BF16),
            pltpu.VMEM((LANES, rows), BF16),
            pltpu.VMEM((LANES, rows), BF16),
            pltpu.VMEM((LANES, rows), BF16),
            pltpu.VMEM((LANES, rows), BF16),
            pltpu.VMEM((LANES, pack * rows), BF16),
            pltpu.VMEM((LANES, pack * rows), BF16),
            pltpu.SemaphoreType.DMA((7, 2, chunks)),
            pltpu.SemaphoreType.DMA((7, 2, chunks)),
            pltpu.SemaphoreType.DMA((3, chunks)),
        ],
        compiler_params=pltpu.CompilerParams(
            collective_id=0, has_side_effects=True, vmem_limit_bytes=56 * 1024 * 1024
        ),
        name="graph_attention",
    )(neighbors, counts, query, key_in, value, grad_out)
    return pl.pallas_call(
        hand_over,
        out_shape=(shape,) * 4,
        in_specs=[hbm] * 4,
        out_specs=(hbm,) * 4,
        scratch_shapes=[
            pltpu.VMEM((4, rows, width), query.dtype),
            pltpu.SemaphoreType.DMA((2, 4)),
        ],
        compiler_params=pltpu.CompilerParams(vmem_limit_bytes=60 * 1024 * 1024),
        name="hand_over",
    )(*results)


def solution(mesh):
    rows = P(("groups", "blk"), None)
    return jax.shard_map(
        functools.partial(local, mesh.shape["blk"]),
        mesh=mesh,
        in_specs=(rows, rows, rows, rows, rows, P(("groups", "blk"))),
        out_specs=(rows,) * 4,
        check_vma=False,
    )
```

```python
import functools
import math

import jax
import jax.numpy as jnp
from jax import lax
from jax.experimental import pallas as pl
from jax.experimental.pallas import tpu as pltpu
from jax.sharding import PartitionSpec as P

HEADS = 16
LANES = 128
AHEAD = 4
SLOTS = 5
MASKED = -1e30
F32 = jnp.float32
BF16 = jnp.bfloat16


def matmul(a, b):
    return jnp.dot(a, b, preferred_element_type=F32)


def matmul_nt(a, b):
    return lax.dot_general(a, b, (((1,), (1,)), ((), ())), preferred_element_type=F32)


def kernel(
    shards, own_blocks, list_width, head_dim,
    nbr_ref, cnt_ref, q_ref, k_ref, v_ref, g_ref,
    out_ref, dq_ref, dk_ref, dv_ref,
    kv, acc, sib_s, sib_r, far_s, far_r, near_s, near_r,
    bias, s_scr, e_scr, d_scr, kt_scr, vt_scr, q_scr, g_scr,
    q_t, g_t, out_t, dq_t, qs_scr, gs_scr, sends, recvs, loads,
):
    rows, width = q_ref.shape
    chunks = width // LANES
    pack = LANES // head_dim
    blk_len = rows // own_blocks
    factor = 1.0 / math.sqrt(head_dim)
    chips = shards // 2

    me = lax.axis_index("blk")
    core = lax.rem(me, 2)
    chip = lax.div(me, 2)
    odd = lax.rem(chip, 2)
    step = 1 - 2 * odd
    near_chip = chip + step
    far_chip = lax.rem(chip - step + chips, chips)
    ahead_chip = lax.rem(chip + 2 * step + chips, chips)
    back_chip = lax.rem(chip - 2 * step + chips, chips)
    sibling = 2 * chip + 1 - core
    near = 2 * near_chip + core
    ahead = 2 * ahead_chip + core
    back = 2 * back_chip + core
    mix = lax.rem(core + chip, 2)
    lent = 2 + mix

    barrier = pltpu.get_barrier_semaphore()
    for other in (sibling, near, ahead, back):
        pl.semaphore_signal(
            barrier, inc=1, device_id={"blk": other}, device_id_type=pl.DeviceIdType.MESH
        )

    def load(which, c):
        cols = pl.ds(pl.multiple_of(c * LANES, LANES), LANES)
        source = (k_ref, v_ref)[which]
        return pltpu.make_async_copy(
            source.at[:, cols], kv.at[0, c, which], loads.at[which, c]
        )

    load_q = pltpu.make_async_copy(q_ref, q_scr, loads.at[2, 0])
    load_g = pltpu.make_async_copy(g_ref, g_scr, loads.at[2, 1])
    for c in range(chunks):
        load(0, c).start()
        load(1, c).start()
    load_q.start()
    load_g.start()

    row_id = lax.broadcasted_iota(jnp.int32, bias.shape, 0)
    lane_blk = lax.broadcasted_iota(jnp.int32, bias.shape, 1) // blk_len
    borrowed_chip = near_chip * mix + far_chip * (1 - mix)
    borrowed = 2 * borrowed_chip + 1 - core
    key_blk = jnp.full(bias.shape, -2, jnp.int32)
    for slot, dev in enumerate((me, sibling, near, 2 * far_chip + core, borrowed)):
        for b in range(own_blocks):
            key_blk = jnp.where(row_id == slot * own_blocks + b, dev * own_blocks + b, key_blk)
    allowed = jnp.zeros(bias.shape, jnp.int32)
    for s in range(list_width):
        entry = jnp.full(bias.shape, -1, jnp.int32)
        for b in range(own_blocks):
            live = jnp.where(s < cnt_ref[b], nbr_ref[b, s], -1)
            entry = jnp.where(lane_blk == b, live, entry)
        allowed = jnp.where(entry == key_blk, 1, allowed)
    bias[...] = jnp.where(allowed == 1, 0.0, MASKED).astype(F32)

    pl.semaphore_wait(barrier, 4)

    def remote(stream, src, dst, c, part, dev):
        return pltpu.make_async_remote_copy(
            src_ref=src,
            dst_ref=dst,
            send_sem=sends.at[stream, part, c],
            recv_sem=recvs.at[stream, part, c],
            device_id={"blk": dev},
            device_id_type=pl.DeviceIdType.MESH,
        )

    def to_near(c, part):
        return remote(0, kv.at[0, c, part], kv.at[2, c, part], c, part, near)

    def to_sibling(c, part):
        return remote(1, kv.at[0, c, part], kv.at[1, c, part], c, part, sibling)

    def relay(c, part):
        return remote(2, kv.at[2, c, part], kv.at[3, c, part], c, part, ahead)

    def lend(c, part):
        return remote(3, kv.at[lent, c, part], kv.at[4, c, part], c, part, sibling)

    def grad_sibling(c, part):
        return remote(4, sib_s.at[c, part], sib_r.at[c, part], c, part, sibling)

    def grad_far(c, part):
        return remote(5, far_s.at[c, part], far_r.at[c, part], c, part, back)

    def grad_near(c, part):
        return remote(6, near_s.at[c, part], near_r.at[c, part], c, part, near)

    def columns(c):
        return pl.ds(pl.multiple_of(c * LANES, LANES), LANES)

    def publish(c):
        for part in range(2):
            load(part, c).wait()
            to_near(c, part).start()
            to_sibling(c, part).start()

    def pass_on(c):
        for part in range(2):
            to_near(c, part).wait_recv()
            relay(c, part).start()

    def lend_on(c):
        for part in range(2):
            relay(c, part).wait_recv()
            lend(c, part).start()

    def send_far(c):
        for part in range(2):
            grad_sibling(c, part).wait_recv()
            acc[c, lent - 1, part] += sib_r[c, part, 1].astype(F32)
            far_s[c, part] = acc[c, 2, part].astype(BF16)
            grad_far(c, part).start()

    def send_near(c):
        for part in range(2):
            grad_far(c, part).wait_recv()
            near_s[c, part] = (acc[c, 1, part] + far_r[c, part].astype(F32)).astype(BF16)
            grad_near(c, part).start()

    def close(c):
        for part, result in enumerate((dk_ref, dv_ref)):
            grad_near(c, part).wait_recv()
            final = acc[c, 0, part] + sib_r[c, part, 0].astype(F32)
            result[:, columns(c)] = (final + near_r[c, part].astype(F32)).astype(BF16)

    def exchange(c):
        for extra in range(2):
            @pl.when(2 * c + extra + AHEAD < chunks)
            def _():
                publish(2 * c + extra + AHEAD)

        for extra in range(2):
            @pl.when(2 * c + extra + 2 < chunks)
            def _():
                pass_on(2 * c + extra + 2)

            @pl.when(2 * c + extra + 1 < chunks)
            def _():
                lend_on(2 * c + extra + 1)

        @pl.when(c >= 1)
        def _():
            send_far(c - 1)

        @pl.when(c >= 2)
        def _():
            send_near(c - 2)

        @pl.when(c >= 3)
        def _():
            close(c - 3)

    def padded(x, h):
        pieces = []
        if h:
            pieces.append(jnp.zeros((h * head_dim, rows), x.dtype))
        pieces.append(x)
        if h < pack - 1:
            pieces.append(jnp.zeros(((pack - 1 - h) * head_dim, rows), x.dtype))
        return jnp.concatenate(pieces, axis=0)

    def one_head(c, h):
        head = slice(h * head_dim, (h + 1) * head_dim)
        here = slice(h * rows, (h + 1) * rows)
        keys = kv[:, c, 0].reshape(SLOTS * rows, LANES)
        vals = kv[:, c, 1].reshape(SLOTS * rows, LANES)
        q_h = q_t[head, :]
        g_h = g_t[head, :]
        s_scr[h] = matmul(keys, padded(q_h, h))
        top = None
        for r in range(SLOTS * own_blocks):
            part = jnp.max(s_scr[h, r * blk_len:(r + 1) * blk_len, :], axis=0, keepdims=True)
            part = part + bias[r:r + 1, :]
            top = part if top is None else jnp.maximum(top, part)
        total = jnp.zeros((1, rows), F32)
        for r in range(SLOTS * own_blocks):
            at = slice(r * blk_len, (r + 1) * blk_len)
            shift = top - bias[r:r + 1, :]
            e = jnp.exp2((s_scr[h, at, :] - shift) * (factor * math.log2(math.e)))
            total = total + jnp.sum(e, axis=0, keepdims=True)
            e_scr[at, here] = e.astype(BF16)
        mixed = matmul(vt_scr[head, :], e_scr[:, here])
        inv = 1.0 / total
        out_h = (mixed * inv).astype(BF16)
        g_f = g_h.astype(F32)
        delta = jnp.sum(g_f * out_h.astype(F32), axis=0, keepdims=True)
        dprobs = matmul(vals, padded(g_h, h))
        d_scr[:, here] = (e_scr[:, here].astype(F32) * (dprobs - delta)).astype(BF16)
        dq = matmul(kt_scr[head, :], d_scr[:, here])
        out_t[head, :] = out_h
        dq_t[head, :] = (dq * (inv * factor)).astype(BF16)
        gs_scr[:, here] = padded((g_f * inv).astype(BF16), h)
        qs_scr[:, here] = padded((q_h.astype(F32) * (inv * factor)).astype(BF16), h)

    for c in range(AHEAD):
        publish(c)
    load_q.wait()
    load_g.wait()
    pass_on(0)
    pass_on(1)
    lend_on(0)

    def body(c, carry):
        cols = columns(c)
        q_t[...] = q_scr[:, cols].T
        g_t[...] = g_scr[:, cols].T
        for part in range(2):
            to_sibling(c, part).wait_recv()
            lend(c, part).wait_recv()
        for slot in range(SLOTS):
            at = slice(slot * rows, (slot + 1) * rows)
            kt_scr[:, at] = kv[slot, c, 0].T
            vt_scr[:, at] = kv[slot, c, 1].T
        for h in range(pack):
            if h == pack // 2:
                exchange(c)
            one_head(c, h)
        for part, (left, right) in enumerate(((d_scr, qs_scr), (e_scr, gs_scr))):
            grad = matmul_nt(left[...], right[...])
            for slot in range(SLOTS):
                at = slice(slot * rows, (slot + 1) * rows)
                if slot in (1, 4):
                    sib_s[c, part, slot // 4] = grad[at].astype(BF16)
                else:
                    acc[c, max(slot - 1, 0), part] = grad[at]
            grad_sibling(c, part).start()
        out_ref[:, cols] = out_t[...].T
        dq_ref[:, cols] = dq_t[...].T
        return carry

    lax.fori_loop(0, chunks, body, 0)

    send_far(chunks - 1)
    send_near(chunks - 2)
    close(chunks - 3)
    send_near(chunks - 1)
    close(chunks - 2)
    close(chunks - 1)

    def finish(c, carry):
        for copy in (to_near, to_sibling, relay, lend, grad_sibling, grad_far, grad_near):
            for part in range(2):
                copy(c, part).wait_send()
        return carry

    lax.fori_loop(0, chunks, finish, 0)


def hand_over(*refs):
    sources, results, held, sems = refs[:4], refs[4:8], refs[8], refs[9]
    reads = [pltpu.make_async_copy(sources[i], held.at[i], sems.at[0, i]) for i in range(4)]
    writes = [pltpu.make_async_copy(held.at[i], results[i], sems.at[1, i]) for i in range(4)]
    for read in reads:
        read.start()
    for read, write in zip(reads, writes):
        read.wait()
        write.start()
    for write in writes:
        write.wait()


def local(shards, query, key_in, value, grad_out, neighbors, counts):
    rows, width = query.shape
    own_blocks, list_width = neighbors.shape
    head_dim = width // HEADS
    chunks = width // LANES
    pack = LANES // head_dim
    tile = (2, rows, LANES)
    vmem = pl.BlockSpec(memory_space=pltpu.VMEM)
    hbm = pl.BlockSpec(memory_space=pl.ANY)
    smem = pl.BlockSpec(memory_space=pltpu.SMEM)
    shape = jax.ShapeDtypeStruct((rows, width), query.dtype)
    bias_rows = -(-SLOTS * own_blocks // 8) * 8
    results = pl.pallas_call(
        functools.partial(kernel, shards, own_blocks, list_width, head_dim),
        out_shape=(shape,) * 4,
        in_specs=[smem, smem, hbm, hbm, hbm, hbm],
        out_specs=(vmem,) * 4,
        scratch_shapes=[
            pltpu.VMEM((SLOTS, chunks) + tile, BF16),
            pltpu.VMEM((chunks, 3) + tile, F32),
            pltpu.VMEM((chunks, 2) + tile, BF16),
            pltpu.VMEM((chunks, 2) + tile, BF16),
            pltpu.VMEM((chunks,) + tile, BF16),
            pltpu.VMEM((chunks,) + tile, BF16),
            pltpu.VMEM((chunks,) + tile, BF16),
            pltpu.VMEM((chunks,) + tile, BF16),
            pltpu.VMEM((bias_rows, rows), F32),
            pltpu.VMEM((pack, SLOTS * rows, rows), F32),
            pltpu.VMEM((SLOTS * rows, pack * rows), BF16),
            pltpu.VMEM((SLOTS * rows, pack * rows), BF16),
            pltpu.VMEM((LANES, SLOTS * rows), BF16),
            pltpu.VMEM((LANES, SLOTS * rows), BF16),
            pltpu.VMEM((rows, width), BF16),
            pltpu.VMEM((rows, width), BF16),
            pltpu.VMEM((LANES, rows), BF16),
            pltpu.VMEM((LANES, rows), BF16),
            pltpu.VMEM((LANES, rows), BF16),
            pltpu.VMEM((LANES, rows), BF16),
            pltpu.VMEM((LANES, pack * rows), BF16),
            pltpu.VMEM((LANES, pack * rows), BF16),
            pltpu.SemaphoreType.DMA((7, 2, chunks)),
            pltpu.SemaphoreType.DMA((7, 2, chunks)),
            pltpu.SemaphoreType.DMA((3, chunks)),
        ],
        compiler_params=pltpu.CompilerParams(
            collective_id=0, has_side_effects=True, vmem_limit_bytes=56 * 1024 * 1024
        ),
        name="graph_attention",
    )(neighbors, counts, query, key_in, value, grad_out)
    return pl.pallas_call(
        hand_over,
        out_shape=(shape,) * 4,
        in_specs=[hbm] * 4,
        out_specs=(hbm,) * 4,
        scratch_shapes=[
            pltpu.VMEM((4, rows, width), query.dtype),
            pltpu.SemaphoreType.DMA((2, 4)),
        ],
        compiler_params=pltpu.CompilerParams(vmem_limit_bytes=60 * 1024 * 1024),
        name="hand_over",
    )(*results)


def solution(mesh):
    rows = P(("groups", "blk"), None)
    return jax.shard_map(
        functools.partial(local, mesh.shape["blk"]),
        mesh=mesh,
        in_specs=(rows, rows, rows, rows, rows, P(("groups", "blk"))),
        out_specs=(rows,) * 4,
        check_vma=False,
    )
```

```python
import functools
import math

import jax
import jax.numpy as jnp
from jax import lax
from jax.experimental import pallas as pl
from jax.experimental.pallas import tpu as pltpu
from jax.sharding import PartitionSpec as P

HEADS = 16
LANES = 128
AHEAD = 3
SLOTS = 5
MASKED = -1e30
F32 = jnp.float32
BF16 = jnp.bfloat16


def matmul(a, b):
    return jnp.dot(a, b, preferred_element_type=F32)


def matmul_nt(a, b):
    return lax.dot_general(a, b, (((1,), (1,)), ((), ())), preferred_element_type=F32)


def kernel(
    shards, own_blocks, list_width, head_dim,
    nbr_ref, cnt_ref, q_ref, k_ref, v_ref, g_ref,
    out_ref, dq_ref, dk_ref, dv_ref,
    kv, acc, sib_s, sib_r, far_s, far_r, near_s, near_r,
    bias, s_scr, e_scr, d_scr, kt_scr, vt_scr, q_scr, g_scr,
    q_t, g_t, out_t, dq_t, qs_scr, gs_scr, qp_scr, gp_scr, sum_scr, sends, recvs, loads,
):
    rows, width = q_ref.shape
    chunks = width // LANES
    pack = LANES // head_dim
    blk_len = rows // own_blocks
    factor = 1.0 / math.sqrt(head_dim)
    chips = shards // 2

    me = lax.axis_index("blk")
    core = lax.rem(me, 2)
    chip = lax.div(me, 2)
    odd = lax.rem(chip, 2)
    step = 1 - 2 * odd
    near_chip = chip + step
    far_chip = lax.rem(chip - step + chips, chips)
    ahead_chip = lax.rem(chip + 2 * step + chips, chips)
    back_chip = lax.rem(chip - 2 * step + chips, chips)
    sibling = 2 * chip + 1 - core
    near = 2 * near_chip + core
    ahead = 2 * ahead_chip + core
    back = 2 * back_chip + core
    mix = lax.rem(core + chip, 2)
    lent = 2 + mix

    barrier = pltpu.get_barrier_semaphore()
    for other in (sibling, near, ahead, back):
        pl.semaphore_signal(
            barrier, inc=1, device_id={"blk": other}, device_id_type=pl.DeviceIdType.MESH
        )

    def load(which, c):
        cols = pl.ds(pl.multiple_of(c * LANES, LANES), LANES)
        source = (k_ref, v_ref)[which]
        return pltpu.make_async_copy(
            source.at[:, cols], kv.at[0, c, which], loads.at[which, c]
        )

    load_q = pltpu.make_async_copy(q_ref, q_scr, loads.at[2, 0])
    load_g = pltpu.make_async_copy(g_ref, g_scr, loads.at[2, 1])
    for c in range(chunks):
        load(0, c).start()
        load(1, c).start()
    load_q.start()
    load_g.start()

    row_id = lax.broadcasted_iota(jnp.int32, bias.shape, 0)
    lane_blk = lax.broadcasted_iota(jnp.int32, bias.shape, 1) // blk_len
    borrowed_chip = near_chip * mix + far_chip * (1 - mix)
    borrowed = 2 * borrowed_chip + 1 - core
    key_blk = jnp.full(bias.shape, -2, jnp.int32)
    for slot, dev in enumerate((me, sibling, near, 2 * far_chip + core, borrowed)):
        for b in range(own_blocks):
            key_blk = jnp.where(row_id == slot * own_blocks + b, dev * own_blocks + b, key_blk)
    allowed = jnp.zeros(bias.shape, jnp.int32)
    for s in range(list_width):
        entry = jnp.full(bias.shape, -1, jnp.int32)
        for b in range(own_blocks):
            live = jnp.where(s < cnt_ref[b], nbr_ref[b, s], -1)
            entry = jnp.where(lane_blk == b, live, entry)
        allowed = jnp.where(entry == key_blk, 1, allowed)
    bias[...] = jnp.where(allowed == 1, 0.0, MASKED).astype(F32)

    for ref in (qp_scr, gp_scr, qs_scr, gs_scr):
        ref[...] = jnp.zeros(ref.shape, BF16)
    vt_scr[...] = jnp.ones(vt_scr.shape, BF16)

    pl.semaphore_wait(barrier, 4)

    def remote(stream, src, dst, c, part, dev):
        return pltpu.make_async_remote_copy(
            src_ref=src,
            dst_ref=dst,
            send_sem=sends.at[stream, part, c],
            recv_sem=recvs.at[stream, part, c],
            device_id={"blk": dev},
            device_id_type=pl.DeviceIdType.MESH,
        )

    def to_near(c, part):
        return remote(0, kv.at[0, c, part], kv.at[2, c, part], c, part, near)

    def to_sibling(c, part):
        return remote(1, kv.at[0, c, part], kv.at[1, c, part], c, part, sibling)

    def relay(c, part):
        return remote(2, kv.at[2, c, part], kv.at[3, c, part], c, part, ahead)

    def lend(c, part):
        return remote(3, kv.at[lent, c, part], kv.at[4, c, part], c, part, sibling)

    def grad_sibling(c, part):
        return remote(4, sib_s.at[c, part], sib_r.at[c, part], c, part, sibling)

    def grad_far(c, part):
        return remote(5, far_s.at[c, part], far_r.at[c, part], c, part, back)

    def grad_near(c, part):
        return remote(6, near_s.at[c, part], near_r.at[c, part], c, part, near)

    def columns(c):
        return pl.ds(pl.multiple_of(c * LANES, LANES), LANES)

    def publish(c):
        for part in range(2):
            load(part, c).wait()
            to_near(c, part).start()
            to_sibling(c, part).start()

    def pass_on(c):
        for part in range(2):
            to_near(c, part).wait_recv()
            relay(c, part).start()

    def lend_on(c):
        for part in range(2):
            relay(c, part).wait_recv()
            lend(c, part).start()

    def send_far(c):
        for part in range(2):
            grad_sibling(c, part).wait_recv()
            acc[c, lent - 1, part] += sib_r[c, part, 1].astype(F32)
            far_s[c, part] = acc[c, 2, part].astype(BF16)
            grad_far(c, part).start()

    def send_near(c):
        for part in range(2):
            grad_far(c, part).wait_recv()
            near_s[c, part] = (acc[c, 1, part] + far_r[c, part].astype(F32)).astype(BF16)
            grad_near(c, part).start()

    def close(c):
        for part, result in enumerate((dk_ref, dv_ref)):
            grad_near(c, part).wait_recv()
            final = acc[c, 0, part] + sib_r[c, part, 0].astype(F32)
            result[:, columns(c)] = (final + near_r[c, part].astype(F32)).astype(BF16)

    def exchange(c):
        @pl.when(c + AHEAD < chunks)
        def _():
            publish(c + AHEAD)

        @pl.when(c + 2 < chunks)
        def _():
            pass_on(c + 2)

        @pl.when(c + 1 < chunks)
        def _():
            lend_on(c + 1)

        @pl.when(c >= 1)
        def _():
            send_far(c - 1)

        @pl.when(c >= 2)
        def _():
            send_near(c - 2)

        @pl.when(c >= 3)
        def _():
            close(c - 3)

    heads = [slice(h * head_dim, (h + 1) * head_dim) for h in range(pack)]
    lanes = [slice(h * rows, (h + 1) * rows) for h in range(pack)]
    spans = [slice(slot * rows, (slot + 1) * rows) for slot in range(SLOTS)]

    def score(c, slot, h, state):
        scores = matmul(kv[slot, c, 0], qp_scr[:, lanes[h]])
        s_scr[h, spans[slot], :] = scores
        for b in range(own_blocks):
            r = slot * own_blocks + b
            part = jnp.max(scores[b * blk_len:(b + 1) * blk_len], axis=0, keepdims=True)
            part = part + bias[r:r + 1, :]
            state["top"] = jnp.maximum(state["top"], part) if slot or b else part

    def weigh(c, slot, h, state):
        for b in range(own_blocks):
            r = slot * own_blocks + b
            at = slice(r * blk_len, (r + 1) * blk_len)
            shift = state["top"] - bias[r:r + 1, :]
            e = jnp.exp2((s_scr[h, at, :] - shift) * (factor * math.log2(math.e)))
            e_scr[at, lanes[h]] = e.astype(BF16)
        term = matmul(vt_scr[h, :, spans[slot]], e_scr[spans[slot], lanes[h]])
        state["mixed"] = state["mixed"] + term if slot else term

    def settle(c, h, state):
        inv = 1.0 / state["mixed"][head_dim:head_dim + 1]
        out_h = (state["mixed"][:head_dim] * inv).astype(BF16)
        g_f = g_t[heads[h], :].astype(F32)
        state["delta"] = jnp.sum(g_f * out_h.astype(F32), axis=0, keepdims=True)
        state["inv"] = inv
        out_t[heads[h], :] = out_h
        gs_scr[heads[h], lanes[h]] = (g_f * inv).astype(BF16)
        qs_scr[heads[h], lanes[h]] = (q_t[heads[h], :].astype(F32) * (inv * factor)).astype(BF16)

    def reverse(c, slot, h, state):
        dprobs = matmul(kv[slot, c, 1], gp_scr[:, lanes[h]])
        d_b = e_scr[spans[slot], lanes[h]] * (dprobs - state["delta"]).astype(BF16)
        d_scr[spans[slot], lanes[h]] = d_b
        term = matmul(kt_scr[heads[h], spans[slot]], d_b)
        state["dq"] = state["dq"] + term if slot else term
        if slot == SLOTS - 1:
            dq_t[heads[h], :] = (state["dq"] * (state["inv"] * factor)).astype(BF16)

    def gather(c, slot, h):
        for part, (left, right) in enumerate(((d_scr, qs_scr), (e_scr, gs_scr))):
            grad = matmul_nt(left[spans[slot], lanes[h]], right[:, lanes[h]])
            if h:
                grad = grad + sum_scr[part, spans[slot], :]
            if h < pack - 1:
                sum_scr[part, spans[slot], :] = grad
            elif slot in (1, 4):
                sib_s[c, part, slot // 4] = grad.astype(BF16)
            else:
                acc[c, max(slot - 1, 0), part] = grad

    for c in range(AHEAD):
        publish(c)
    load_q.wait()
    load_g.wait()
    pass_on(0)
    pass_on(1)
    lend_on(0)

    def body(c, carry):
        cols = columns(c)
        q_t[...] = q_scr[:, cols].T
        g_t[...] = g_scr[:, cols].T
        for h in range(pack):
            qp_scr[heads[h], lanes[h]] = q_t[heads[h], :]
            gp_scr[heads[h], lanes[h]] = g_t[heads[h], :]
        for part in range(2):
            to_sibling(c, part).wait_recv()
            lend(c, part).wait_recv()
        states = [{} for _ in range(pack)]
        for step in range(pack + 3):
            if step == 2:
                exchange(c)
            for slot in range(SLOTS):
                if step == 0:
                    v_t = kv[slot, c, 1].T
                    for h in range(pack):
                        vt_scr[h, :head_dim, spans[slot]] = v_t[heads[h]]
                if step == 1:
                    kt_scr[:, spans[slot]] = kv[slot, c, 0].T
                for h in range(pack):
                    at = step - h
                    if at == 0:
                        score(c, slot, h, states[h])
                    elif at == 1:
                        weigh(c, slot, h, states[h])
                    elif at == 2:
                        if slot == 0:
                            settle(c, h, states[h])
                        reverse(c, slot, h, states[h])
                    elif at == 3:
                        gather(c, slot, h)
        for part in range(2):
            grad_sibling(c, part).start()
        out_ref[:, cols] = out_t[...].T
        dq_ref[:, cols] = dq_t[...].T
        return carry

    lax.fori_loop(0, chunks, body, 0)

    send_far(chunks - 1)
    send_near(chunks - 2)
    close(chunks - 3)
    send_near(chunks - 1)
    close(chunks - 2)
    close(chunks - 1)

    def finish(c, carry):
        for copy in (to_near, to_sibling, relay, lend, grad_sibling, grad_far, grad_near):
            for part in range(2):
                copy(c, part).wait_send()
        return carry

    lax.fori_loop(0, chunks, finish, 0)


def hand_over(*refs):
    sources, results, held, sems = refs[:4], refs[4:8], refs[8], refs[9]
    reads = [pltpu.make_async_copy(sources[i], held.at[i], sems.at[0, i]) for i in range(4)]
    writes = [pltpu.make_async_copy(held.at[i], results[i], sems.at[1, i]) for i in range(4)]
    for read in reads:
        read.start()
    for read, write in zip(reads, writes):
        read.wait()
        write.start()
    for write in writes:
        write.wait()


def local(shards, query, key_in, value, grad_out, neighbors, counts):
    rows, width = query.shape
    own_blocks, list_width = neighbors.shape
    head_dim = width // HEADS
    chunks = width // LANES
    pack = LANES // head_dim
    tile = (2, rows, LANES)
    vmem = pl.BlockSpec(memory_space=pltpu.VMEM)
    hbm = pl.BlockSpec(memory_space=pl.ANY)
    smem = pl.BlockSpec(memory_space=pltpu.SMEM)
    shape = jax.ShapeDtypeStruct((rows, width), query.dtype)
    bias_rows = -(-SLOTS * own_blocks // 8) * 8
    results = pl.pallas_call(
        functools.partial(kernel, shards, own_blocks, list_width, head_dim),
        out_shape=(shape,) * 4,
        in_specs=[smem, smem, hbm, hbm, hbm, hbm],
        out_specs=(vmem,) * 4,
        scratch_shapes=[
            pltpu.VMEM((SLOTS, chunks) + tile, BF16),
            pltpu.VMEM((chunks, 3) + tile, F32),
            pltpu.VMEM((chunks, 2) + tile, BF16),
            pltpu.VMEM((chunks, 2) + tile, BF16),
            pltpu.VMEM((chunks,) + tile, BF16),
            pltpu.VMEM((chunks,) + tile, BF16),
            pltpu.VMEM((chunks,) + tile, BF16),
            pltpu.VMEM((chunks,) + tile, BF16),
            pltpu.VMEM((bias_rows, rows), F32),
            pltpu.VMEM((pack, SLOTS * rows, rows), F32),
            pltpu.VMEM((SLOTS * rows, pack * rows), BF16),
            pltpu.VMEM((SLOTS * rows, pack * rows), BF16),
            pltpu.VMEM((LANES, SLOTS * rows), BF16),
            pltpu.VMEM((pack, head_dim + 16, SLOTS * rows), BF16),
            pltpu.VMEM((rows, width), BF16),
            pltpu.VMEM((rows, width), BF16),
            pltpu.VMEM((LANES, rows), BF16),
            pltpu.VMEM((LANES, rows), BF16),
            pltpu.VMEM((LANES, rows), BF16),
            pltpu.VMEM((LANES, rows), BF16),
            pltpu.VMEM((LANES, pack * rows), BF16),
            pltpu.VMEM((LANES, pack * rows), BF16),
            pltpu.VMEM((LANES, pack * rows), BF16),
            pltpu.VMEM((LANES, pack * rows), BF16),
            pltpu.VMEM((2, SLOTS * rows, LANES), F32),
            pltpu.SemaphoreType.DMA((7, 2, chunks)),
            pltpu.SemaphoreType.DMA((7, 2, chunks)),
            pltpu.SemaphoreType.DMA((3, chunks)),
        ],
        compiler_params=pltpu.CompilerParams(
            collective_id=0, has_side_effects=True, vmem_limit_bytes=56 * 1024 * 1024
        ),
        name="graph_attention",
    )(neighbors, counts, query, key_in, value, grad_out)
    return pl.pallas_call(
        hand_over,
        out_shape=(shape,) * 4,
        in_specs=[hbm] * 4,
        out_specs=(hbm,) * 4,
        scratch_shapes=[
            pltpu.VMEM((4, rows, width), query.dtype),
            pltpu.SemaphoreType.DMA((2, 4)),
        ],
        compiler_params=pltpu.CompilerParams(vmem_limit_bytes=60 * 1024 * 1024),
        name="hand_over",
    )(*results)


def solution(mesh):
    rows = P(("groups", "blk"), None)
    return jax.shard_map(
        functools.partial(local, mesh.shape["blk"]),
        mesh=mesh,
        in_specs=(rows, rows, rows, rows, rows, P(("groups", "blk"))),
        out_specs=(rows,) * 4,
        check_vma=False,
    )
```

```python
import functools
import math

import jax
import jax.numpy as jnp
from jax import lax
from jax.experimental import pallas as pl
from jax.experimental.pallas import tpu as pltpu
from jax.sharding import PartitionSpec as P

HEADS = 16
LANES = 128
AHEAD = 3
SLOTS = 5
MASKED = -1e30
F32 = jnp.float32
BF16 = jnp.bfloat16


def matmul(a, b):
    return jnp.dot(a, b, preferred_element_type=F32)


def matmul_nt(a, b):
    return lax.dot_general(a, b, (((1,), (1,)), ((), ())), preferred_element_type=F32)


def kernel(
    shards, own_blocks, list_width, head_dim,
    nbr_ref, cnt_ref, q_ref, k_ref, v_ref, g_ref,
    out_ref, dq_ref, dk_ref, dv_ref,
    kv, acc, sib_s, sib_r, far_s, far_r, near_s, near_r,
    bias, s_scr, e_scr, d_scr, kt_scr, vt_scr, q_scr, g_scr,
    q_t, g_t, out_t, dq_t, qs_scr, gs_scr, qp_scr, gp_scr, sum_scr, sends, recvs, loads,
):
    rows, width = q_ref.shape
    chunks = width // LANES
    pack = LANES // head_dim
    blk_len = rows // own_blocks
    factor = 1.0 / math.sqrt(head_dim)
    chips = shards // 2

    me = lax.axis_index("blk")
    core = lax.rem(me, 2)
    chip = lax.div(me, 2)
    odd = lax.rem(chip, 2)
    step = 1 - 2 * odd
    near_chip = chip + step
    far_chip = lax.rem(chip - step + chips, chips)
    ahead_chip = lax.rem(chip + 2 * step + chips, chips)
    back_chip = lax.rem(chip - 2 * step + chips, chips)
    sibling = 2 * chip + 1 - core
    near = 2 * near_chip + core
    ahead = 2 * ahead_chip + core
    back = 2 * back_chip + core
    mix = lax.rem(core + chip, 2)
    lent = 2 + mix

    barrier = pltpu.get_barrier_semaphore()
    for other in (sibling, near, ahead, back):
        pl.semaphore_signal(
            barrier, inc=1, device_id={"blk": other}, device_id_type=pl.DeviceIdType.MESH
        )

    def load(which, c):
        cols = pl.ds(pl.multiple_of(c * LANES, LANES), LANES)
        source = (k_ref, v_ref)[which]
        return pltpu.make_async_copy(
            source.at[:, cols], kv.at[0, c, which], loads.at[which, c]
        )

    load_q = pltpu.make_async_copy(q_ref, q_scr, loads.at[2, 0])
    load_g = pltpu.make_async_copy(g_ref, g_scr, loads.at[2, 1])
    for c in range(chunks):
        load(0, c).start()
        load(1, c).start()
    load_q.start()
    load_g.start()

    row_id = lax.broadcasted_iota(jnp.int32, bias.shape, 0)
    lane_blk = lax.broadcasted_iota(jnp.int32, bias.shape, 1) // blk_len
    borrowed_chip = near_chip * mix + far_chip * (1 - mix)
    borrowed = 2 * borrowed_chip + 1 - core
    key_blk = jnp.full(bias.shape, -2, jnp.int32)
    for slot, dev in enumerate((me, sibling, near, 2 * far_chip + core, borrowed)):
        for b in range(own_blocks):
            key_blk = jnp.where(row_id == slot * own_blocks + b, dev * own_blocks + b, key_blk)
    allowed = jnp.zeros(bias.shape, jnp.int32)
    for s in range(list_width):
        entry = jnp.full(bias.shape, -1, jnp.int32)
        for b in range(own_blocks):
            live = jnp.where(s < cnt_ref[b], nbr_ref[b, s], -1)
            entry = jnp.where(lane_blk == b, live, entry)
        allowed = jnp.where(entry == key_blk, 1, allowed)
    bias[...] = jnp.where(allowed == 1, 0.0, MASKED).astype(F32)

    for ref in (qp_scr, gp_scr, qs_scr, gs_scr):
        ref[...] = jnp.zeros(ref.shape, BF16)
    vt_scr[...] = jnp.ones(vt_scr.shape, BF16)

    pl.semaphore_wait(barrier, 4)

    def remote(stream, src, dst, c, part, dev):
        return pltpu.make_async_remote_copy(
            src_ref=src,
            dst_ref=dst,
            send_sem=sends.at[stream, part, c],
            recv_sem=recvs.at[stream, part, c],
            device_id={"blk": dev},
            device_id_type=pl.DeviceIdType.MESH,
        )

    def to_near(c, part):
        return remote(0, kv.at[0, c, part], kv.at[2, c, part], c, part, near)

    def to_sibling(c, part):
        return remote(1, kv.at[0, c, part], kv.at[1, c, part], c, part, sibling)

    def relay(c, part):
        return remote(2, kv.at[2, c, part], kv.at[3, c, part], c, part, ahead)

    def lend(c, part):
        return remote(3, kv.at[lent, c, part], kv.at[4, c, part], c, part, sibling)

    def grad_sibling(c, part):
        return remote(4, sib_s.at[c, part], sib_r.at[c, part], c, part, sibling)

    def grad_far(c, part):
        return remote(5, far_s.at[c, part], far_r.at[c, part], c, part, back)

    def grad_near(c, part):
        return remote(6, near_s.at[c, part], near_r.at[c, part], c, part, near)

    def columns(c):
        return pl.ds(pl.multiple_of(c * LANES, LANES), LANES)

    def publish_part(c, part):
        load(part, c).wait()
        to_near(c, part).start()
        to_sibling(c, part).start()

    def publish(c):
        for part in range(2):
            publish_part(c, part)

    def pass_part(c, part):
        to_near(c, part).wait_recv()
        relay(c, part).start()

    def pass_on(c):
        for part in range(2):
            pass_part(c, part)

    def lend_on(c):
        for part in range(2):
            relay(c, part).wait_recv()
            lend(c, part).start()

    def send_far(c):
        for part in range(2):
            grad_sibling(c, part).wait_recv()
            acc[c, lent - 1, part] += sib_r[c, part, 1].astype(F32)
            far_s[c, part] = acc[c, 2, part].astype(BF16)
            grad_far(c, part).start()

    def send_near(c):
        for part in range(2):
            grad_far(c, part).wait_recv()
            near_s[c, part] = (acc[c, 1, part] + far_r[c, part].astype(F32)).astype(BF16)
            grad_near(c, part).start()

    def close(c):
        for part, result in enumerate((dk_ref, dv_ref)):
            grad_near(c, part).wait_recv()
            final = acc[c, 0, part] + sib_r[c, part, 0].astype(F32)
            result[:, columns(c)] = (final + near_r[c, part].astype(F32)).astype(BF16)

    def exchange(c):
        @pl.when(c + AHEAD < chunks)
        def _():
            publish(c + AHEAD)

        @pl.when(c + 2 < chunks)
        def _():
            pass_on(c + 2)

        @pl.when(c + 1 < chunks)
        def _():
            lend_on(c + 1)

        @pl.when(c >= 1)
        def _():
            send_far(c - 1)

        @pl.when(c >= 2)
        def _():
            send_near(c - 2)

        @pl.when(c >= 3)
        def _():
            close(c - 3)

    heads = [slice(h * head_dim, (h + 1) * head_dim) for h in range(pack)]
    lanes = [slice(h * rows, (h + 1) * rows) for h in range(pack)]
    spans = [slice(slot * rows, (slot + 1) * rows) for slot in range(SLOTS)]

    def score(c, slot, h, state):
        scores = matmul(kv[slot, c, 0], qp_scr[:, lanes[h]])
        s_scr[h, spans[slot], :] = scores
        for b in range(own_blocks):
            r = slot * own_blocks + b
            part = jnp.max(scores[b * blk_len:(b + 1) * blk_len], axis=0, keepdims=True)
            part = part + bias[r:r + 1, :]
            state["top"] = jnp.maximum(state["top"], part) if slot or b else part

    def weigh(c, slot, h, state):
        for b in range(own_blocks):
            r = slot * own_blocks + b
            at = slice(r * blk_len, (r + 1) * blk_len)
            shift = state["top"] - bias[r:r + 1, :]
            e = jnp.exp2((s_scr[h, at, :] - shift) * (factor * math.log2(math.e)))
            e_scr[at, lanes[h]] = e.astype(BF16)
        term = matmul(vt_scr[h, :, spans[slot]], e_scr[spans[slot], lanes[h]])
        state["mixed"] = state["mixed"] + term if slot else term

    def settle(c, h, state):
        inv = 1.0 / state["mixed"][head_dim:head_dim + 1]
        out_h = (state["mixed"][:head_dim] * inv).astype(BF16)
        g_f = g_t[heads[h], :].astype(F32)
        state["delta"] = jnp.sum(g_f * out_h.astype(F32), axis=0, keepdims=True)
        state["inv"] = inv
        out_t[heads[h], :] = out_h
        gs_scr[heads[h], lanes[h]] = (g_f * inv).astype(BF16)
        qs_scr[heads[h], lanes[h]] = (q_t[heads[h], :].astype(F32) * (inv * factor)).astype(BF16)

    def reverse(c, slot, h, state):
        dprobs = matmul(kv[slot, c, 1], gp_scr[:, lanes[h]])
        d_b = e_scr[spans[slot], lanes[h]] * (dprobs - state["delta"]).astype(BF16)
        d_scr[spans[slot], lanes[h]] = d_b
        term = matmul(kt_scr[heads[h], spans[slot]], d_b)
        state["dq"] = state["dq"] + term if slot else term
        if slot == SLOTS - 1:
            dq_t[heads[h], :] = (state["dq"] * (state["inv"] * factor)).astype(BF16)

    def gather(c, slot, h):
        for part, (left, right) in enumerate(((d_scr, qs_scr), (e_scr, gs_scr))):
            grad = matmul_nt(left[spans[slot], lanes[h]], right[:, lanes[h]])
            if h:
                grad = grad + sum_scr[part, spans[slot], :]
            if h < pack - 1:
                sum_scr[part, spans[slot], :] = grad
            elif slot in (1, 4):
                sib_s[c, part, slot // 4] = grad.astype(BF16)
            else:
                acc[c, max(slot - 1, 0), part] = grad

    publish(0)
    for c in range(AHEAD - 1):
        for part in range(2):
            pass_part(c, part)
            publish_part(c + 1, part)
    load_q.wait()
    load_g.wait()
    lend_on(0)

    def body(c, carry):
        cols = columns(c)
        q_t[...] = q_scr[:, cols].T
        g_t[...] = g_scr[:, cols].T
        for h in range(pack):
            qp_scr[heads[h], lanes[h]] = q_t[heads[h], :]
            gp_scr[heads[h], lanes[h]] = g_t[heads[h], :]
        for part in range(2):
            to_sibling(c, part).wait_recv()
            lend(c, part).wait_recv()
        states = [{} for _ in range(pack)]
        for step in range(pack + 3):
            if step == 2:
                exchange(c)
            for slot in range(SLOTS):
                if step == 0:
                    v_t = kv[slot, c, 1].T
                    for h in range(pack):
                        vt_scr[h, :head_dim, spans[slot]] = v_t[heads[h]]
                if step == 1:
                    kt_scr[:, spans[slot]] = kv[slot, c, 0].T
                for h in range(pack):
                    at = step - h
                    if at == 0:
                        score(c, slot, h, states[h])
                    elif at == 1:
                        weigh(c, slot, h, states[h])
                    elif at == 2:
                        if slot == 0:
                            settle(c, h, states[h])
                        reverse(c, slot, h, states[h])
                    elif at == 3:
                        gather(c, slot, h)
        for part in range(2):
            grad_sibling(c, part).start()
        out_ref[:, cols] = out_t[...].T
        dq_ref[:, cols] = dq_t[...].T
        return carry

    lax.fori_loop(0, chunks, body, 0)

    send_far(chunks - 1)
    send_near(chunks - 2)
    close(chunks - 3)
    send_near(chunks - 1)
    close(chunks - 2)
    close(chunks - 1)

    def finish(c, carry):
        for copy in (to_near, to_sibling, relay, lend, grad_sibling, grad_far, grad_near):
            for part in range(2):
                copy(c, part).wait_send()
        return carry

    lax.fori_loop(0, chunks, finish, 0)


def hand_over(*refs):
    sources, results, sems = refs[:4], refs[4:8], refs[8]
    copies = [pltpu.make_async_copy(sources[i], results[i], sems.at[i]) for i in range(4)]
    for copy in copies:
        copy.start()
    for copy in copies:
        copy.wait()


def local(shards, query, key_in, value, grad_out, neighbors, counts):
    rows, width = query.shape
    own_blocks, list_width = neighbors.shape
    head_dim = width // HEADS
    chunks = width // LANES
    pack = LANES // head_dim
    tile = (2, rows, LANES)
    vmem = pl.BlockSpec(memory_space=pltpu.VMEM)
    hbm = pl.BlockSpec(memory_space=pl.ANY)
    fixed = pl.BlockSpec(memory_space=pltpu.HBM)
    smem = pl.BlockSpec(memory_space=pltpu.SMEM)
    shape = jax.ShapeDtypeStruct((rows, width), query.dtype)
    bias_rows = -(-SLOTS * own_blocks // 8) * 8
    query, key_in, value, grad_out, neighbors, counts = (
        pltpu.with_memory_space_constraint(x, pltpu.HBM)
        for x in (query, key_in, value, grad_out, neighbors, counts)
    )
    results = pl.pallas_call(
        functools.partial(kernel, shards, own_blocks, list_width, head_dim),
        out_shape=(shape,) * 4,
        in_specs=[smem, smem, fixed, fixed, fixed, fixed],
        out_specs=(vmem,) * 4,
        scratch_shapes=[
            pltpu.VMEM((SLOTS, chunks) + tile, BF16),
            pltpu.VMEM((chunks, 3) + tile, F32),
            pltpu.VMEM((chunks, 2) + tile, BF16),
            pltpu.VMEM((chunks, 2) + tile, BF16),
            pltpu.VMEM((chunks,) + tile, BF16),
            pltpu.VMEM((chunks,) + tile, BF16),
            pltpu.VMEM((chunks,) + tile, BF16),
            pltpu.VMEM((chunks,) + tile, BF16),
            pltpu.VMEM((bias_rows, rows), F32),
            pltpu.VMEM((pack, SLOTS * rows, rows), F32),
            pltpu.VMEM((SLOTS * rows, pack * rows), BF16),
            pltpu.VMEM((SLOTS * rows, pack * rows), BF16),
            pltpu.VMEM((LANES, SLOTS * rows), BF16),
            pltpu.VMEM((pack, head_dim + 16, SLOTS * rows), BF16),
            pltpu.VMEM((rows, width), BF16),
            pltpu.VMEM((rows, width), BF16),
            pltpu.VMEM((LANES, rows), BF16),
            pltpu.VMEM((LANES, rows), BF16),
            pltpu.VMEM((LANES, rows), BF16),
            pltpu.VMEM((LANES, rows), BF16),
            pltpu.VMEM((LANES, pack * rows), BF16),
            pltpu.VMEM((LANES, pack * rows), BF16),
            pltpu.VMEM((LANES, pack * rows), BF16),
            pltpu.VMEM((LANES, pack * rows), BF16),
            pltpu.VMEM((2, SLOTS * rows, LANES), F32),
            pltpu.SemaphoreType.DMA((7, 2, chunks)),
            pltpu.SemaphoreType.DMA((7, 2, chunks)),
            pltpu.SemaphoreType.DMA((3, chunks)),
        ],
        compiler_params=pltpu.CompilerParams(
            collective_id=0, has_side_effects=True, vmem_limit_bytes=40 * 1024 * 1024
        ),
        name="graph_attention",
    )(neighbors, counts, query, key_in, value, grad_out)
    return pl.pallas_call(
        hand_over,
        out_shape=(shape,) * 4,
        in_specs=[vmem] * 4,
        out_specs=(fixed,) * 4,
        scratch_shapes=[
            pltpu.SemaphoreType.DMA((4,)),
        ],
        compiler_params=pltpu.CompilerParams(vmem_limit_bytes=16 * 1024 * 1024),
        name="hand_over",
    )(*results)


def solution(mesh):
    rows = P(("groups", "blk"), None)
    return jax.shard_map(
        functools.partial(local, mesh.shape["blk"]),
        mesh=mesh,
        in_specs=(rows, rows, rows, rows, rows, P(("groups", "blk"))),
        out_specs=(rows,) * 4,
        check_vma=False,
    )
```

```python
import functools
import math

import jax
import jax.numpy as jnp
from jax import lax
from jax.experimental import pallas as pl
from jax.experimental.pallas import tpu as pltpu
from jax.sharding import PartitionSpec as P

HEADS = 16
LANES = 128
AHEAD = 3
SLOTS = 5
MASKED = -1e30
F32 = jnp.float32
BF16 = jnp.bfloat16


def matmul(a, b):
    return jnp.dot(a, b, preferred_element_type=F32)


def matmul_nt(a, b):
    return lax.dot_general(a, b, (((1,), (1,)), ((), ())), preferred_element_type=F32)


def kernel(
    shards, own_blocks, list_width, head_dim,
    nbr_ref, cnt_ref, q_ref, k_ref, v_ref, g_ref,
    out_ref, dq_ref, dk_ref, dv_ref,
    kv, acc, sib_s, sib_r, far_s, far_r, near_s, near_r,
    bias, s_scr, e_scr, d_scr, kt_scr, vt_scr, q_scr, g_scr,
    q_t, g_t, out_t, dq_t, qs_scr, gs_scr, qp_scr, gp_scr, sum_scr, sends, recvs, loads,
):
    rows, width = q_ref.shape
    chunks = width // LANES
    pack = LANES // head_dim
    blk_len = rows // own_blocks
    factor = 1.0 / math.sqrt(head_dim)
    chips = shards // 2

    me = lax.axis_index("blk")
    core = lax.rem(me, 2)
    chip = lax.div(me, 2)
    odd = lax.rem(chip, 2)
    step = 1 - 2 * odd
    near_chip = chip + step
    far_chip = lax.rem(chip - step + chips, chips)
    ahead_chip = lax.rem(chip + 2 * step + chips, chips)
    back_chip = lax.rem(chip - 2 * step + chips, chips)
    sibling = 2 * chip + 1 - core
    near = 2 * near_chip + core
    ahead = 2 * ahead_chip + core
    back = 2 * back_chip + core
    mix = lax.rem(core + chip, 2)
    lent = 2 + mix

    barrier = pltpu.get_barrier_semaphore()
    for other in (sibling, near, ahead, back):
        pl.semaphore_signal(
            barrier, inc=1, device_id={"blk": other}, device_id_type=pl.DeviceIdType.MESH
        )

    def load(which, c):
        cols = pl.ds(pl.multiple_of(c * LANES, LANES), LANES)
        source = (k_ref, v_ref)[which]
        return pltpu.make_async_copy(
            source.at[:, cols], kv.at[0, c, which], loads.at[which, c]
        )

    load_q = pltpu.make_async_copy(q_ref, q_scr, loads.at[2, 0])
    load_g = pltpu.make_async_copy(g_ref, g_scr, loads.at[2, 1])
    for c in range(chunks):
        load(0, c).start()
        load(1, c).start()
    load_q.start()
    load_g.start()

    row_id = lax.broadcasted_iota(jnp.int32, bias.shape, 0)
    lane_blk = lax.broadcasted_iota(jnp.int32, bias.shape, 1) // blk_len
    borrowed_chip = near_chip * mix + far_chip * (1 - mix)
    borrowed = 2 * borrowed_chip + 1 - core
    key_blk = jnp.full(bias.shape, -2, jnp.int32)
    for slot, dev in enumerate((me, sibling, near, 2 * far_chip + core, borrowed)):
        for b in range(own_blocks):
            key_blk = jnp.where(row_id == slot * own_blocks + b, dev * own_blocks + b, key_blk)
    allowed = jnp.zeros(bias.shape, jnp.int32)
    for s in range(list_width):
        entry = jnp.full(bias.shape, -1, jnp.int32)
        for b in range(own_blocks):
            live = jnp.where(s < cnt_ref[b], nbr_ref[b, s], -1)
            entry = jnp.where(lane_blk == b, live, entry)
        allowed = jnp.where(entry == key_blk, 1, allowed)
    bias[...] = jnp.where(allowed == 1, 0.0, MASKED).astype(F32)

    for ref in (qp_scr, gp_scr, qs_scr, gs_scr):
        ref[...] = jnp.zeros(ref.shape, BF16)
    vt_scr[...] = jnp.ones(vt_scr.shape, BF16)

    pl.semaphore_wait(barrier, 4)

    def remote(stream, src, dst, c, part, dev):
        return pltpu.make_async_remote_copy(
            src_ref=src,
            dst_ref=dst,
            send_sem=sends.at[stream, part, c],
            recv_sem=recvs.at[stream, part, c],
            device_id={"blk": dev},
            device_id_type=pl.DeviceIdType.MESH,
        )

    def to_near(c, part):
        return remote(0, kv.at[0, c, part], kv.at[2, c, part], c, part, near)

    def to_sibling(c, part):
        return remote(1, kv.at[0, c, part], kv.at[1, c, part], c, part, sibling)

    def relay(c, part):
        return remote(2, kv.at[2, c, part], kv.at[3, c, part], c, part, ahead)

    def lend(c, part):
        return remote(3, kv.at[lent, c, part], kv.at[4, c, part], c, part, sibling)

    def grad_sibling(c, part):
        return remote(4, sib_s.at[c, part], sib_r.at[c, part], c, part, sibling)

    def grad_far(c, part):
        return remote(5, far_s.at[c, part], far_r.at[c, part], c, part, back)

    def grad_near(c, part):
        return remote(6, near_s.at[c, part], near_r.at[c, part], c, part, near)

    def columns(c):
        return pl.ds(pl.multiple_of(c * LANES, LANES), LANES)

    def publish_part(c, part):
        load(part, c).wait()
        to_near(c, part).start()
        to_sibling(c, part).start()

    def publish(c):
        for part in range(2):
            publish_part(c, part)

    def pass_part(c, part):
        to_near(c, part).wait_recv()
        relay(c, part).start()

    def pass_on(c):
        for part in range(2):
            pass_part(c, part)

    def lend_on(c):
        for part in range(2):
            relay(c, part).wait_recv()
            lend(c, part).start()

    def send_far(c):
        for part in range(2):
            grad_sibling(c, part).wait_recv()
            acc[c, lent - 1, part] += sib_r[c, part, 1].astype(F32)
            far_s[c, part] = acc[c, 2, part].astype(BF16)
            grad_far(c, part).start()

    def send_near(c):
        for part in range(2):
            grad_far(c, part).wait_recv()
            near_s[c, part] = (acc[c, 1, part] + far_r[c, part].astype(F32)).astype(BF16)
            grad_near(c, part).start()

    def close(c):
        for part, result in enumerate((dk_ref, dv_ref)):
            grad_near(c, part).wait_recv()
            final = acc[c, 0, part] + sib_r[c, part, 0].astype(F32)
            result[:, columns(c)] = (final + near_r[c, part].astype(F32)).astype(BF16)

    def exchange(c):
        @pl.when(c + AHEAD < chunks)
        def _():
            publish(c + AHEAD)

        @pl.when(c >= 1)
        def _():
            send_far(c - 1)

        @pl.when(c >= 2)
        def _():
            send_near(c - 2)

        @pl.when(c + 2 < chunks)
        def _():
            pass_on(c + 2)

        @pl.when(c + 1 < chunks)
        def _():
            lend_on(c + 1)

        @pl.when(c >= 3)
        def _():
            close(c - 3)

    heads = [slice(h * head_dim, (h + 1) * head_dim) for h in range(pack)]
    lanes = [slice(h * rows, (h + 1) * rows) for h in range(pack)]
    spans = [slice(slot * rows, (slot + 1) * rows) for slot in range(SLOTS)]

    def score(c, slot, h, state):
        scores = matmul(kv[slot, c, 0], qp_scr[:, lanes[h]])
        s_scr[h, spans[slot], :] = scores
        for b in range(own_blocks):
            r = slot * own_blocks + b
            part = jnp.max(scores[b * blk_len:(b + 1) * blk_len], axis=0, keepdims=True)
            part = part + bias[r:r + 1, :]
            state["top"] = jnp.maximum(state["top"], part) if slot or b else part

    def weigh(c, slot, h, state):
        for b in range(own_blocks):
            r = slot * own_blocks + b
            at = slice(r * blk_len, (r + 1) * blk_len)
            shift = state["top"] - bias[r:r + 1, :]
            e = jnp.exp2((s_scr[h, at, :] - shift) * (factor * math.log2(math.e)))
            e_scr[at, lanes[h]] = e.astype(BF16)
        term = matmul(vt_scr[h, :, spans[slot]], e_scr[spans[slot], lanes[h]])
        state["mixed"] = state["mixed"] + term if slot else term

    def settle(c, h, state):
        inv = 1.0 / state["mixed"][head_dim:head_dim + 1]
        out_h = (state["mixed"][:head_dim] * inv).astype(BF16)
        g_f = g_t[heads[h], :].astype(F32)
        state["delta"] = jnp.sum(g_f * out_h.astype(F32), axis=0, keepdims=True)
        state["inv"] = inv
        out_t[heads[h], :] = out_h
        gs_scr[heads[h], lanes[h]] = (g_f * inv).astype(BF16)
        qs_scr[heads[h], lanes[h]] = (q_t[heads[h], :].astype(F32) * (inv * factor)).astype(BF16)

    def reverse(c, slot, h, state):
        dprobs = matmul(kv[slot, c, 1], gp_scr[:, lanes[h]])
        d_b = e_scr[spans[slot], lanes[h]] * (dprobs - state["delta"]).astype(BF16)
        d_scr[spans[slot], lanes[h]] = d_b
        term = matmul(kt_scr[heads[h], spans[slot]], d_b)
        state["dq"] = state["dq"] + term if slot else term
        if slot == SLOTS - 1:
            dq_t[heads[h], :] = (state["dq"] * (state["inv"] * factor)).astype(BF16)

    def gather(c, slot, h):
        for part, (left, right) in enumerate(((d_scr, qs_scr), (e_scr, gs_scr))):
            grad = matmul_nt(left[spans[slot], lanes[h]], right[:, lanes[h]])
            if h:
                grad = grad + sum_scr[part, spans[slot], :]
            if h < pack - 1:
                sum_scr[part, spans[slot], :] = grad
            elif slot in (1, 4):
                sib_s[c, part, slot // 4] = grad.astype(BF16)
            else:
                acc[c, max(slot - 1, 0), part] = grad

    publish(0)
    for c in range(AHEAD - 1):
        for part in range(2):
            pass_part(c, part)
            publish_part(c + 1, part)
    load_q.wait()
    load_g.wait()
    lend_on(0)

    def body(c, carry):
        cols = columns(c)
        q_t[...] = q_scr[:, cols].T
        g_t[...] = g_scr[:, cols].T
        for h in range(pack):
            qp_scr[heads[h], lanes[h]] = q_t[heads[h], :]
            gp_scr[heads[h], lanes[h]] = g_t[heads[h], :]
        for part in range(2):
            to_sibling(c, part).wait_recv()
            lend(c, part).wait_recv()
        states = [{} for _ in range(pack)]
        for step in range(pack + 3):
            if step == 2:
                exchange(c)
            for slot in (1, 4, 0, 2, 3) if step == pack + 2 else range(SLOTS):
                if step == 0:
                    v_t = kv[slot, c, 1].T
                    for h in range(pack):
                        vt_scr[h, :head_dim, spans[slot]] = v_t[heads[h]]
                if step == 1:
                    kt_scr[:, spans[slot]] = kv[slot, c, 0].T
                for h in range(pack):
                    at = step - h
                    if at == 0:
                        score(c, slot, h, states[h])
                    elif at == 1:
                        weigh(c, slot, h, states[h])
                    elif at == 2:
                        if slot == 0:
                            settle(c, h, states[h])
                        reverse(c, slot, h, states[h])
                    elif at == 3:
                        gather(c, slot, h)
                if step == pack + 2 and slot == 4:
                    for part in range(2):
                        grad_sibling(c, part).start()
        out_ref[:, cols] = out_t[...].T
        dq_ref[:, cols] = dq_t[...].T
        return carry

    lax.fori_loop(0, chunks, body, 0)

    send_far(chunks - 1)
    send_near(chunks - 2)
    close(chunks - 3)
    send_near(chunks - 1)
    close(chunks - 2)
    close(chunks - 1)

    def finish(c, carry):
        for copy in (to_near, to_sibling, relay, lend, grad_sibling, grad_far, grad_near):
            for part in range(2):
                copy(c, part).wait_send()
        return carry

    lax.fori_loop(0, chunks, finish, 0)


def hand_over(*refs):
    sources, results, sems = refs[:4], refs[4:8], refs[8]
    copies = [pltpu.make_async_copy(sources[i], results[i], sems.at[i]) for i in range(4)]
    for copy in copies:
        copy.start()
    for copy in copies:
        copy.wait()


def local(shards, query, key_in, value, grad_out, neighbors, counts):
    rows, width = query.shape
    own_blocks, list_width = neighbors.shape
    head_dim = width // HEADS
    chunks = width // LANES
    pack = LANES // head_dim
    tile = (2, rows, LANES)
    vmem = pl.BlockSpec(memory_space=pltpu.VMEM)
    hbm = pl.BlockSpec(memory_space=pl.ANY)
    fixed = pl.BlockSpec(memory_space=pltpu.HBM)
    smem = pl.BlockSpec(memory_space=pltpu.SMEM)
    shape = jax.ShapeDtypeStruct((rows, width), query.dtype)
    bias_rows = -(-SLOTS * own_blocks // 8) * 8
    query, key_in, value, grad_out, neighbors, counts = (
        pltpu.with_memory_space_constraint(x, pltpu.HBM)
        for x in (query, key_in, value, grad_out, neighbors, counts)
    )
    results = pl.pallas_call(
        functools.partial(kernel, shards, own_blocks, list_width, head_dim),
        out_shape=(shape,) * 4,
        in_specs=[smem, smem, fixed, fixed, fixed, fixed],
        out_specs=(vmem,) * 4,
        scratch_shapes=[
            pltpu.VMEM((SLOTS, chunks) + tile, BF16),
            pltpu.VMEM((chunks, 3) + tile, F32),
            pltpu.VMEM((chunks, 2) + tile, BF16),
            pltpu.VMEM((chunks, 2) + tile, BF16),
            pltpu.VMEM((chunks,) + tile, BF16),
            pltpu.VMEM((chunks,) + tile, BF16),
            pltpu.VMEM((chunks,) + tile, BF16),
            pltpu.VMEM((chunks,) + tile, BF16),
            pltpu.VMEM((bias_rows, rows), F32),
            pltpu.VMEM((pack, SLOTS * rows, rows), F32),
            pltpu.VMEM((SLOTS * rows, pack * rows), BF16),
            pltpu.VMEM((SLOTS * rows, pack * rows), BF16),
            pltpu.VMEM((LANES, SLOTS * rows), BF16),
            pltpu.VMEM((pack, head_dim + 16, SLOTS * rows), BF16),
            pltpu.VMEM((rows, width), BF16),
            pltpu.VMEM((rows, width), BF16),
            pltpu.VMEM((LANES, rows), BF16),
            pltpu.VMEM((LANES, rows), BF16),
            pltpu.VMEM((LANES, rows), BF16),
            pltpu.VMEM((LANES, rows), BF16),
            pltpu.VMEM((LANES, pack * rows), BF16),
            pltpu.VMEM((LANES, pack * rows), BF16),
            pltpu.VMEM((LANES, pack * rows), BF16),
            pltpu.VMEM((LANES, pack * rows), BF16),
            pltpu.VMEM((2, SLOTS * rows, LANES), F32),
            pltpu.SemaphoreType.DMA((7, 2, chunks)),
            pltpu.SemaphoreType.DMA((7, 2, chunks)),
            pltpu.SemaphoreType.DMA((3, chunks)),
        ],
        compiler_params=pltpu.CompilerParams(
            collective_id=0, has_side_effects=True, vmem_limit_bytes=40 * 1024 * 1024
        ),
        name="graph_attention",
    )(neighbors, counts, query, key_in, value, grad_out)
    return pl.pallas_call(
        hand_over,
        out_shape=(shape,) * 4,
        in_specs=[vmem] * 4,
        out_specs=(fixed,) * 4,
        scratch_shapes=[
            pltpu.SemaphoreType.DMA((4,)),
        ],
        compiler_params=pltpu.CompilerParams(vmem_limit_bytes=16 * 1024 * 1024),
        name="hand_over",
    )(*results)


def solution(mesh):
    rows = P(("groups", "blk"), None)
    return jax.shard_map(
        functools.partial(local, mesh.shape["blk"]),
        mesh=mesh,
        in_specs=(rows, rows, rows, rows, rows, P(("groups", "blk"))),
        out_specs=(rows,) * 4,
        check_vma=False,
    )
```

```python
import functools
import math

import jax
import jax.numpy as jnp
from jax import lax
from jax.experimental import pallas as pl
from jax.experimental.pallas import tpu as pltpu
from jax.sharding import PartitionSpec as P

HEADS = 16
LANES = 128
AHEAD = 3
SLOTS = 5
MASKED = -1e30
F32 = jnp.float32
BF16 = jnp.bfloat16


def matmul(a, b):
    return jnp.dot(a, b, preferred_element_type=F32)


def matmul_nt(a, b):
    return lax.dot_general(a, b, (((1,), (1,)), ((), ())), preferred_element_type=F32)


def kernel(
    shards, own_blocks, list_width, head_dim,
    nbr_ref, cnt_ref, q_ref, k_ref, v_ref, g_ref,
    out_ref, dq_ref, dk_ref, dv_ref,
    kv, acc, sib_s, sib_r, far_s, far_r, near_s, near_r,
    bias, s_scr, e_scr, d_scr, kt_scr, vt_scr, q_scr, g_scr,
    q_t, g_t, out_t, dq_t, qs_scr, gs_scr, qp_scr, gp_scr, sum_scr, sends, recvs, loads,
):
    rows, width = q_ref.shape
    chunks = width // LANES
    pack = LANES // head_dim
    blk_len = rows // own_blocks
    factor = 1.0 / math.sqrt(head_dim)
    chips = shards // 2

    me = lax.axis_index("blk")
    core = lax.rem(me, 2)
    chip = lax.div(me, 2)
    odd = lax.rem(chip, 2)
    step = 1 - 2 * odd
    near_chip = chip + step
    far_chip = lax.rem(chip - step + chips, chips)
    ahead_chip = lax.rem(chip + 2 * step + chips, chips)
    back_chip = lax.rem(chip - 2 * step + chips, chips)
    sibling = 2 * chip + 1 - core
    near = 2 * near_chip + core
    ahead = 2 * ahead_chip + core
    back = 2 * back_chip + core
    mix = lax.rem(core + chip, 2)
    lent = 2 + mix

    barrier = pltpu.get_barrier_semaphore()
    for other in (sibling, near, ahead, back):
        pl.semaphore_signal(
            barrier, inc=1, device_id={"blk": other}, device_id_type=pl.DeviceIdType.MESH
        )

    def load(which, c):
        cols = pl.ds(pl.multiple_of(c * LANES, LANES), LANES)
        source = (k_ref, v_ref)[which]
        return pltpu.make_async_copy(
            source.at[:, cols], kv.at[0, c, which], loads.at[which, c]
        )

    load_q = pltpu.make_async_copy(q_ref, q_scr, loads.at[2, 0])
    load_g = pltpu.make_async_copy(g_ref, g_scr, loads.at[2, 1])
    for c in range(chunks):
        load(0, c).start()
        load(1, c).start()
    load_q.start()
    load_g.start()

    row_id = lax.broadcasted_iota(jnp.int32, bias.shape, 0)
    lane_blk = lax.broadcasted_iota(jnp.int32, bias.shape, 1) // blk_len
    borrowed_chip = near_chip * mix + far_chip * (1 - mix)
    borrowed = 2 * borrowed_chip + 1 - core
    key_blk = jnp.full(bias.shape, -2, jnp.int32)
    for slot, dev in enumerate((me, sibling, near, 2 * far_chip + core, borrowed)):
        for b in range(own_blocks):
            key_blk = jnp.where(row_id == slot * own_blocks + b, dev * own_blocks + b, key_blk)
    allowed = jnp.zeros(bias.shape, jnp.int32)
    for s in range(list_width):
        entry = jnp.full(bias.shape, -1, jnp.int32)
        for b in range(own_blocks):
            live = jnp.where(s < cnt_ref[b], nbr_ref[b, s], -1)
            entry = jnp.where(lane_blk == b, live, entry)
        allowed = jnp.where(entry == key_blk, 1, allowed)
    bias[...] = jnp.where(allowed == 1, 0.0, MASKED).astype(F32)

    for ref in (qp_scr, gp_scr, qs_scr, gs_scr):
        ref[...] = jnp.zeros(ref.shape, BF16)
    vt_scr[...] = jnp.ones(vt_scr.shape, BF16)

    pl.semaphore_wait(barrier, 4)

    def remote(stream, src, dst, c, part, dev):
        return pltpu.make_async_remote_copy(
            src_ref=src,
            dst_ref=dst,
            send_sem=sends.at[stream, part, c],
            recv_sem=recvs.at[stream, part, c],
            device_id={"blk": dev},
            device_id_type=pl.DeviceIdType.MESH,
        )

    def to_near(c, part):
        return remote(0, kv.at[0, c, part], kv.at[2, c, part], c, part, near)

    def to_sibling(c, part):
        return remote(1, kv.at[0, c, part], kv.at[1, c, part], c, part, sibling)

    def relay(c, part):
        return remote(2, kv.at[2, c, part], kv.at[3, c, part], c, part, ahead)

    def lend(c, part):
        return remote(3, kv.at[lent, c, part], kv.at[4, c, part], c, part, sibling)

    def grad_sibling(c, part):
        return remote(4, sib_s.at[c, part], sib_r.at[c, part], c, part, sibling)

    def grad_far(c, part):
        return remote(5, far_s.at[c, part], far_r.at[c, part], c, part, back)

    def grad_near(c, part):
        return remote(6, near_s.at[c, part], near_r.at[c, part], c, part, near)

    def columns(c):
        return pl.ds(pl.multiple_of(c * LANES, LANES), LANES)

    def publish_part(c, part):
        load(part, c).wait()
        to_near(c, part).start()
        to_sibling(c, part).start()

    def publish(c):
        for part in range(2):
            publish_part(c, part)

    def pass_part(c, part):
        to_near(c, part).wait_recv()
        relay(c, part).start()

    def pass_on(c):
        for part in range(2):
            pass_part(c, part)

    def lend_on(c):
        for part in range(2):
            relay(c, part).wait_recv()
            lend(c, part).start()

    def send_far(c):
        for part in range(2):
            grad_sibling(c, part).wait_recv()
            acc[c, lent - 1, part] += sib_r[c, part, 1].astype(F32)
            far_s[c, part] = acc[c, 2, part].astype(BF16)
            grad_far(c, part).start()

    def send_near(c):
        for part in range(2):
            grad_far(c, part).wait_recv()
            near_s[c, part] = (acc[c, 1, part] + far_r[c, part].astype(F32)).astype(BF16)
            grad_near(c, part).start()

    def close(c):
        for part, result in enumerate((dk_ref, dv_ref)):
            grad_near(c, part).wait_recv()
            final = acc[c, 0, part] + sib_r[c, part, 0].astype(F32)
            result[:, columns(c)] = (final + near_r[c, part].astype(F32)).astype(BF16)

    def exchange(c):
        @pl.when(c + AHEAD < chunks)
        def _():
            publish(c + AHEAD)

        @pl.when(c + 2 < chunks)
        def _():
            pass_on(c + 2)

        @pl.when(c + 1 < chunks)
        def _():
            lend_on(c + 1)

    def exchange_grads(c):
        @pl.when(c >= 1)
        def _():
            send_far(c - 1)

        @pl.when(c >= 2)
        def _():
            send_near(c - 2)

        @pl.when(c >= 3)
        def _():
            close(c - 3)

    heads = [slice(h * head_dim, (h + 1) * head_dim) for h in range(pack)]
    lanes = [slice(h * rows, (h + 1) * rows) for h in range(pack)]
    spans = [slice(slot * rows, (slot + 1) * rows) for slot in range(SLOTS)]

    def score(c, slot, h, state):
        scores = matmul(kv[slot, c, 0], qp_scr[:, lanes[h]])
        s_scr[h, spans[slot], :] = scores
        for b in range(own_blocks):
            r = slot * own_blocks + b
            part = jnp.max(scores[b * blk_len:(b + 1) * blk_len], axis=0, keepdims=True)
            part = part + bias[r:r + 1, :]
            state["top"] = jnp.maximum(state["top"], part) if slot or b else part

    def weigh(c, slot, h, state):
        for b in range(own_blocks):
            r = slot * own_blocks + b
            at = slice(r * blk_len, (r + 1) * blk_len)
            shift = state["top"] - bias[r:r + 1, :]
            e = jnp.exp2((s_scr[h, at, :] - shift) * (factor * math.log2(math.e)))
            e_scr[at, lanes[h]] = e.astype(BF16)
        term = matmul(vt_scr[h, :, spans[slot]], e_scr[spans[slot], lanes[h]])
        state["mixed"] = state["mixed"] + term if slot else term

    def settle(c, h, state):
        inv = 1.0 / state["mixed"][head_dim:head_dim + 1]
        out_h = (state["mixed"][:head_dim] * inv).astype(BF16)
        g_f = g_t[heads[h], :].astype(F32)
        state["delta"] = jnp.sum(g_f * out_h.astype(F32), axis=0, keepdims=True)
        state["inv"] = inv
        out_t[heads[h], :] = out_h
        gs_scr[heads[h], lanes[h]] = (g_f * inv).astype(BF16)
        qs_scr[heads[h], lanes[h]] = (q_t[heads[h], :].astype(F32) * (inv * factor)).astype(BF16)

    def reverse(c, slot, h, state):
        dprobs = matmul(kv[slot, c, 1], gp_scr[:, lanes[h]])
        d_b = e_scr[spans[slot], lanes[h]] * (dprobs - state["delta"]).astype(BF16)
        d_scr[spans[slot], lanes[h]] = d_b
        term = matmul(kt_scr[heads[h], spans[slot]], d_b)
        state["dq"] = state["dq"] + term if slot else term
        if slot == SLOTS - 1:
            dq_t[heads[h], :] = (state["dq"] * (state["inv"] * factor)).astype(BF16)

    def gather(c, slot, h):
        for part, (left, right) in enumerate(((d_scr, qs_scr), (e_scr, gs_scr))):
            grad = matmul_nt(left[spans[slot], lanes[h]], right[:, lanes[h]])
            if h:
                grad = grad + sum_scr[part, spans[slot], :]
            if h < pack - 1:
                sum_scr[part, spans[slot], :] = grad
            elif slot in (1, 4):
                sib_s[c, part, slot // 4] = grad.astype(BF16)
            else:
                acc[c, max(slot - 1, 0), part] = grad

    publish(0)
    for c in range(AHEAD - 1):
        for part in range(2):
            pass_part(c, part)
            publish_part(c + 1, part)
    load_q.wait()
    load_g.wait()
    lend_on(0)

    def body(c, carry):
        cols = columns(c)
        q_t[...] = q_scr[:, cols].T
        g_t[...] = g_scr[:, cols].T
        for h in range(pack):
            qp_scr[heads[h], lanes[h]] = q_t[heads[h], :]
            gp_scr[heads[h], lanes[h]] = g_t[heads[h], :]
        for part in range(2):
            to_sibling(c, part).wait_recv()
            lend(c, part).wait_recv()
        states = [{} for _ in range(pack)]
        for step in range(pack + 3):
            if step == 1:
                exchange(c)
            if step == 3:
                exchange_grads(c)
            for slot in range(SLOTS):
                if step == 0:
                    v_t = kv[slot, c, 1].T
                    for h in range(pack):
                        vt_scr[h, :head_dim, spans[slot]] = v_t[heads[h]]
                if step == 1:
                    kt_scr[:, spans[slot]] = kv[slot, c, 0].T
                for h in range(pack):
                    at = step - h
                    if at == 0:
                        score(c, slot, h, states[h])
                    elif at == 1:
                        weigh(c, slot, h, states[h])
                    elif at == 2:
                        if slot == 0:
                            settle(c, h, states[h])
                        reverse(c, slot, h, states[h])
                    elif at == 3:
                        gather(c, slot, h)
        for part in range(2):
            grad_sibling(c, part).start()
        out_ref[:, cols] = out_t[...].T
        dq_ref[:, cols] = dq_t[...].T
        return carry

    lax.fori_loop(0, chunks, body, 0)

    send_far(chunks - 1)
    send_near(chunks - 2)
    close(chunks - 3)
    send_near(chunks - 1)
    close(chunks - 2)
    close(chunks - 1)

    def finish(c, carry):
        for copy in (to_near, to_sibling, relay, lend, grad_sibling, grad_far, grad_near):
            for part in range(2):
                copy(c, part).wait_send()
        return carry

    lax.fori_loop(0, chunks, finish, 0)


def hand_over(*refs):
    sources, results, sems = refs[:4], refs[4:8], refs[8]
    copies = [pltpu.make_async_copy(sources[i], results[i], sems.at[i]) for i in range(4)]
    for copy in copies:
        copy.start()
    for copy in copies:
        copy.wait()


def local(shards, query, key_in, value, grad_out, neighbors, counts):
    rows, width = query.shape
    own_blocks, list_width = neighbors.shape
    head_dim = width // HEADS
    chunks = width // LANES
    pack = LANES // head_dim
    tile = (2, rows, LANES)
    vmem = pl.BlockSpec(memory_space=pltpu.VMEM)
    hbm = pl.BlockSpec(memory_space=pl.ANY)
    fixed = pl.BlockSpec(memory_space=pltpu.HBM)
    smem = pl.BlockSpec(memory_space=pltpu.SMEM)
    shape = jax.ShapeDtypeStruct((rows, width), query.dtype)
    bias_rows = -(-SLOTS * own_blocks // 8) * 8
    query, key_in, value, grad_out, neighbors, counts = (
        pltpu.with_memory_space_constraint(x, pltpu.HBM)
        for x in (query, key_in, value, grad_out, neighbors, counts)
    )
    results = pl.pallas_call(
        functools.partial(kernel, shards, own_blocks, list_width, head_dim),
        out_shape=(shape,) * 4,
        in_specs=[smem, smem, fixed, fixed, fixed, fixed],
        out_specs=(vmem,) * 4,
        scratch_shapes=[
            pltpu.VMEM((SLOTS, chunks) + tile, BF16),
            pltpu.VMEM((chunks, 3) + tile, F32),
            pltpu.VMEM((chunks, 2) + tile, BF16),
            pltpu.VMEM((chunks, 2) + tile, BF16),
            pltpu.VMEM((chunks,) + tile, BF16),
            pltpu.VMEM((chunks,) + tile, BF16),
            pltpu.VMEM((chunks,) + tile, BF16),
            pltpu.VMEM((chunks,) + tile, BF16),
            pltpu.VMEM((bias_rows, rows), F32),
            pltpu.VMEM((pack, SLOTS * rows, rows), F32),
            pltpu.VMEM((SLOTS * rows, pack * rows), BF16),
            pltpu.VMEM((SLOTS * rows, pack * rows), BF16),
            pltpu.VMEM((LANES, SLOTS * rows), BF16),
            pltpu.VMEM((pack, head_dim + 16, SLOTS * rows), BF16),
            pltpu.VMEM((rows, width), BF16),
            pltpu.VMEM((rows, width), BF16),
            pltpu.VMEM((LANES, rows), BF16),
            pltpu.VMEM((LANES, rows), BF16),
            pltpu.VMEM((LANES, rows), BF16),
            pltpu.VMEM((LANES, rows), BF16),
            pltpu.VMEM((LANES, pack * rows), BF16),
            pltpu.VMEM((LANES, pack * rows), BF16),
            pltpu.VMEM((LANES, pack * rows), BF16),
            pltpu.VMEM((LANES, pack * rows), BF16),
            pltpu.VMEM((2, SLOTS * rows, LANES), F32),
            pltpu.SemaphoreType.DMA((7, 2, chunks)),
            pltpu.SemaphoreType.DMA((7, 2, chunks)),
            pltpu.SemaphoreType.DMA((3, chunks)),
        ],
        compiler_params=pltpu.CompilerParams(
            collective_id=0, has_side_effects=True, vmem_limit_bytes=40 * 1024 * 1024
        ),
        name="graph_attention",
    )(neighbors, counts, query, key_in, value, grad_out)
    return pl.pallas_call(
        hand_over,
        out_shape=(shape,) * 4,
        in_specs=[vmem] * 4,
        out_specs=(fixed,) * 4,
        scratch_shapes=[
            pltpu.SemaphoreType.DMA((4,)),
        ],
        compiler_params=pltpu.CompilerParams(vmem_limit_bytes=16 * 1024 * 1024),
        name="hand_over",
    )(*results)


def solution(mesh):
    rows = P(("groups", "blk"), None)
    return jax.shard_map(
        functools.partial(local, mesh.shape["blk"]),
        mesh=mesh,
        in_specs=(rows, rows, rows, rows, rows, P(("groups", "blk"))),
        out_specs=(rows,) * 4,
        check_vma=False,
    )
```
